128 devices in a mesh: seq: 16 (over y, x_hi, core), tp: 8 (over z, x_lo).
Axes of the slice: x: 4 (x_hi: 2, x_lo: 2; x = x_hi * 2 + x_lo), y: 4, z: 4, core: 2. Of those that a mesh axis runs over, the one named last changes fastest.
Arguments:
- resid: bfloat16 [32, 8192], P(None, 'seq'), may hold values from -40 to 40
- attn_gain: bfloat16 [8192], P('seq'), may hold values from 0.5 to 1.5
- ffn_gain: bfloat16 [8192], P('seq'), may hold values from 0.5 to 1.5
- w_query: bfloat16 [8192, 8192], P('seq', 'tp'), may hold values from -0.0625 to 0.0625
- w_key: bfloat16 [8192, 1024], P('seq', 'tp'), may hold values from -0.625 to 0.625
- w_value: bfloat16 [8192, 1024], P('seq', 'tp'), may hold values from -0.0625 to 0.0625
- w_out: bfloat16 [8192, 8192], P('tp', 'seq'), may hold values from -0.0625 to 0.0625
- rope_angle: float32 [32, 64], replicated, may hold values from -3.140625 to 3.140625
- positions: int32 [32], replicated, may hold values from 0 to 31
- cache_keys: bfloat16 [8, 262144, 128], P('tp', 'seq'), may hold values from -210 to 210
- cache_values: bfloat16 [8, 262144, 128], P('tp', 'seq'), may hold values from -6 to 6
- valid_lengths: int32 [16], P('seq'), may hold values from 1 to 16384, 196608 in all
- w_gate: bfloat16 [8192, 28672], P('seq', 'tp'), may hold values from -0.0625 to 0.0625
- w_up: bfloat16 [8192, 28672], P('seq', 'tp'), may hold values from -0.0625 to 0.0625
- w_down: bfloat16 [28672, 8192], P('tp', 'seq'), may hold values from -0.03125 to 0.03125
Outputs:
- attn_out: bfloat16 [32, 8192], P(None, 'seq')
- layer_out: bfloat16 [32, 8192], P(None, 'seq')
The draws below stay inside these ranges and needn't reach their ends.
Inputs may be any that keep to these rules, and one draw needn't show every extreme that they name: `valid_lengths`: each block's valid tokens fill its first slots; at least one block is full.
All inputs are finite; a program needn't handle non-finite values.
Results may differ from the reference program's by a relative error of at most 0.012.
The reference program's roundings to bfloat16 on the way count: a program that leaves them out, or rounds other values in their place, can miss the bound.
Values may be sent and summed in bfloat16 or wider, within the bound.
No kernel may reach another device: no remote copies, remote signals or barrier semaphores. Data moves between devices by JAX's collectives and lax.ppermute only.
A program may use at most 128 MiB of HBM per device.

```python
import math
import jax
import jax.numpy as jnp
import numpy as np
from jax import lax

D = 8192
HEADS = 64
KV_HEADS = 8
HD = 128
FF = 28672
QB = 32
CACHE_DEV = 16384
CACHE = 262144
N_SEQ = 16


def draw_resid(key, part):
    key = jax.random.fold_in(key, 11)
    key_base, key_rows = jax.random.split(key, 2)
    columns = 0.3 * 10.0 ** (jnp.arange(D, dtype=jnp.float32) / max(D - 1, 1))
    row_scale = 0.2 * 10.0 ** jax.random.uniform(key_rows, (QB, 1), jnp.float32)
    base = jnp.clip(jax.random.normal(key_base, (QB, D), jnp.float32), -6.0, 6.0)
    return (base * columns[None, :] * row_scale).astype(jnp.bfloat16)


def draw_cache_keys(key, part):
    key = jax.random.fold_in(key, 23)
    base = jnp.clip(3.0 * jax.random.normal(key, (KV_HEADS, CACHE, HD), jnp.float32), -15.0, 15.0)
    return base.astype(jnp.bfloat16)


def plant(array, rng, least, top_value):
    shape = array.shape
    spot = [jax.random.randint(jax.random.fold_in(rng, axis), (), 0, shape[axis]) for axis in range(len(shape))]
    array = array.at[tuple(spot)].set(least)
    longest = shape.index(max(shape))
    spot[longest] = (spot[longest] + 1) % shape[longest]
    return array.at[tuple(spot)].set(top_value)


def level_of(own_key, shape, cuts, low, top_value):
    gain, own = 1.0, jax.random.fold_in(own_key, 6)
    for axis_at, shards_of in cuts:
        draws = jnp.exp(jax.random.uniform(jax.random.fold_in(own, axis_at), (shards_of,), jnp.float32, low / len(cuts), top_value / len(cuts)))
        gain = gain * jnp.repeat(draws, shape[axis_at] // shards_of).reshape([-1 if axis == axis_at else 1 for axis in range(len(shape))])
    return gain


def profile(number_of, total, limit, skew):
    weights = [(1 << 20) // math.isqrt(grade ** skew) + 1 for grade in range(2, number_of + 1)]
    rest, counts = total - limit - (number_of - 1), [1] * (number_of - 1)
    while rest > 0:
        free = [i for i in range(number_of - 1) if counts[i] < limit]
        mass, left = sum([weights[i] for i in free]), rest
        for i in free:
            extra = min(limit - counts[i], max(1, left * weights[i] // mass), rest)
            counts[i] = counts[i] + extra
            rest = rest - extra
    return np.array([limit] + counts)


def ragged(own_key, amount, total, reach, slope):
    if amount == 2:
        one = jax.random.randint(own_key, (), max(1, total - reach), min(reach, total - 1) + 1)
        return jnp.stack([one, total - one])
    sizes = jnp.asarray(profile(amount, total, reach, slope), jnp.int32)
    pairs = (amount - 1) // 2
    donor, receiver = sizes[1:1 + 2 * pairs:2], sizes[2:2 + 2 * pairs:2]
    margin = jnp.minimum(donor - 1, reach - receiver)
    passed = jax.random.randint(jax.random.fold_in(own_key, 1), (pairs,), 0, 1 << 20) % (margin + 1)
    sizes = sizes.at[1:1 + 2 * pairs:2].set(donor - passed).at[2:2 + 2 * pairs:2].set(receiver + passed)
    return sizes[jax.random.permutation(jax.random.fold_in(own_key, 2), amount)]


def gaussian(rng, shape, scale, bound, pieces=(), kind=jnp.bfloat16):
    array = jax.random.normal(rng, shape, jnp.float32) * scale
    if len(pieces) > 0:
        array = level_of(rng, shape, pieces, -0.22, 0.18) * array
    return jnp.clip(array, min=-bound, max=bound).astype(kind)


def setup_inputs(seed: int = 0) -> dict:
    seeds = jax.random.split(jax.random.key(seed), 16)
    resid = draw_resid(jax.random.fold_in(seeds[15], 71), 0)
    attn_gain = jnp.clip(1.0 + 0.1 * jax.random.normal(seeds[1], (D,), jnp.float32), 0.5, 1.5).astype(jnp.bfloat16)
    ffn_gain = jnp.clip(1.0 + 0.1 * jax.random.normal(seeds[2], (D,), jnp.float32), 0.5, 1.5).astype(jnp.bfloat16)
    w_query = gaussian(seeds[3], (D, HEADS * HD), D ** -0.5, 0.0625, ((0, 16), (1, 8)))
    w_key = gaussian(seeds[4], (D, KV_HEADS * HD), (max(D // 81, 1)) ** -0.5, 0.625, ((0, 16), (1, 8)))
    w_value = gaussian(seeds[5], (D, KV_HEADS * HD), D ** -0.5, 0.0625, ((0, 16), (1, 8)))
    w_out = gaussian(seeds[6], (HEADS * HD, D), (HEADS * HD) ** -0.5, 0.0625, ((0, 8), (1, 16)))
    rope_angle = jnp.clip(jax.random.uniform(seeds[7], (QB, HD // 2), jnp.float32, -3.140625, 3.140625), -3.140625, 3.140625)
    positions = plant(jax.random.randint(seeds[8], (QB,), 0, QB), jax.random.fold_in(seeds[8], 1), 0, QB - 1).astype(jnp.int32)
    cache_keys = draw_cache_keys(jax.random.fold_in(seeds[15], 71), 0)
    cache_values = gaussian(seeds[10], (KV_HEADS, CACHE, HD), 1.0, 6.0, ((0, 8), (1, 16)))
    valid_lengths = ragged(seeds[11], N_SEQ, N_SEQ * CACHE_DEV * 3 // 4, CACHE_DEV, 1).astype(jnp.int32)
    w_gate = gaussian(seeds[12], (D, FF), D ** -0.5, 0.0625, ((0, 16), (1, 8)))
    w_up = gaussian(seeds[13], (D, FF), D ** -0.5, 0.0625, ((0, 16), (1, 8)))
    w_down = gaussian(seeds[14], (FF, D), FF ** -0.5, 0.03125, ((0, 8), (1, 16)))
    return dict(resid=resid, attn_gain=attn_gain, ffn_gain=ffn_gain, w_query=w_query, w_key=w_key, w_value=w_value, w_out=w_out, rope_angle=rope_angle, positions=positions, cache_keys=cache_keys, cache_values=cache_values, valid_lengths=valid_lengths, w_gate=w_gate, w_up=w_up, w_down=w_down)


EPS = 1e-05

def rotate(values, angle):
    half = values.shape[-1] // 2
    cosine = jnp.cos(angle)[:, None, :]
    sine = jnp.sin(angle)[:, None, :]
    first = values[..., :half]
    second = values[..., half:]
    return jnp.concatenate([first * cosine - second * sine, second * cosine + first * sine], axis=-1)

def merge_parts(left, right):
    top = jnp.maximum(left[0], right[0])
    f_left = jnp.exp(left[0] - top)
    f_right = jnp.exp(right[0] - top)
    return (top, left[1] * f_left + right[1] * f_right, left[2] * f_left[..., None] + right[2] * f_right[..., None])

def reference(resid, attn_gain, ffn_gain, w_query, w_key, w_value, w_out, rope_angle, positions, cache_keys, cache_values, valid_lengths, w_gate, w_up, w_down):
    group = HEADS // KV_HEADS
    scale = 1.0 / HD ** 0.5
    resid32 = resid.astype(jnp.float32)
    inv_first = lax.rsqrt(lax.optimization_barrier(jnp.sum(resid32 * resid32, axis=1)) / D + EPS)[:, None]
    normed_in = (resid32 * attn_gain.astype(jnp.float32)).astype(jnp.bfloat16)
    q_full = jnp.dot(normed_in, w_query, preferred_element_type=jnp.float32) * inv_first
    k_full = jnp.dot(normed_in, w_key, preferred_element_type=jnp.float32) * inv_first
    v_full = jnp.dot(normed_in, w_value, preferred_element_type=jnp.float32) * inv_first
    query = rotate(q_full.reshape(QB, HEADS, HD), rope_angle).astype(jnp.bfloat16)
    key_new = rotate(k_full.reshape(QB, KV_HEADS, HD), rope_angle).astype(jnp.bfloat16)
    value_new = v_full.reshape(QB, KV_HEADS, HD).astype(jnp.bfloat16)
    grouped = query.astype(jnp.float32).reshape(QB, KV_HEADS, group, HD)
    keys = cache_keys.reshape(KV_HEADS, N_SEQ, CACHE_DEV, HD)
    values = cache_values.reshape(KV_HEADS, N_SEQ, CACHE_DEV, HD)

    def one_block(index):
        key_block = lax.dynamic_index_in_dim(keys, index, 1, keepdims=False).astype(jnp.float32)
        value_block = lax.dynamic_index_in_dim(values, index, 1, keepdims=False).astype(jnp.float32)
        scores = jnp.einsum('rkgd,ktd->kgrt', grouped, key_block) * scale
        live = jnp.arange(CACHE_DEV, dtype=jnp.int32) < valid_lengths[index]
        scores = jnp.where(live, scores, jnp.float32(-1e+30))
        top = lax.optimization_barrier(jnp.max(scores, axis=-1))
        weights = jnp.exp(scores - top[..., None]).astype(jnp.bfloat16).astype(jnp.float32)
        total = lax.optimization_barrier(jnp.sum(weights, axis=-1))
        summed = jnp.einsum('kgrt,ktd->kgrd', weights, value_block)
        return (top, total, summed)
    tops, totals, sums = lax.map(one_block, jnp.arange(N_SEQ, dtype=jnp.int32))
    top = lax.optimization_barrier(jnp.max(tops, axis=0))
    factor = jnp.exp(tops - top)
    total = lax.optimization_barrier(jnp.sum(factor * totals, axis=0))
    summed = lax.optimization_barrier(jnp.sum(factor[..., None] * sums, axis=0))
    scores = jnp.einsum('rkgd,skd->kgrs', grouped, key_new.astype(jnp.float32)) * scale
    live = positions[None, :] <= positions[:, None]
    scores = jnp.where(live, scores, jnp.float32(-1e+30))
    top_new = lax.optimization_barrier(jnp.max(scores, axis=-1))
    weights = jnp.exp(scores - top_new[..., None]).astype(jnp.bfloat16).astype(jnp.float32)
    total_new = lax.optimization_barrier(jnp.sum(weights, axis=-1))
    summed_new = jnp.einsum('kgrs,skd->kgrd', weights, value_new.astype(jnp.float32))
    top, total, summed = merge_parts((top, total, summed), (top_new, total_new, summed_new))
    attn = (summed / total[..., None]).transpose(2, 0, 1, 3).reshape(QB, HEADS * HD).astype(jnp.bfloat16)
    attn_out = jnp.dot(attn, w_out, preferred_element_type=jnp.float32).astype(jnp.bfloat16)
    hidden_mid = (resid32 + lax.optimization_barrier(attn_out).astype(jnp.float32)).astype(jnp.bfloat16)
    mid32 = lax.optimization_barrier(hidden_mid).astype(jnp.float32)
    inv_second = lax.rsqrt(lax.optimization_barrier(jnp.sum(mid32 * mid32, axis=1)) / D + EPS)[:, None]
    normed_mid = (mid32 * ffn_gain.astype(jnp.float32)).astype(jnp.bfloat16)
    gate = jnp.dot(normed_mid, w_gate, preferred_element_type=jnp.float32) * inv_second
    up = jnp.dot(normed_mid, w_up, preferred_element_type=jnp.float32) * inv_second
    act = (jax.nn.silu(gate) * up).astype(jnp.bfloat16)
    layer_out = (mid32 + jnp.dot(act, w_down, preferred_element_type=jnp.float32)).astype(jnp.bfloat16)
    return (attn_out, layer_out)
```

```python
import functools

import jax
import jax.numpy as jnp
from jax import lax
from jax.experimental import pallas as pl
from jax.experimental.pallas import tpu as pltpu
from jax.sharding import PartitionSpec as P

EPS = 1e-05
LOW = -1e30
TINY = 1e-30
FULL = 32766.0
F32 = jnp.float32
BF16 = jnp.bfloat16
LANES = 128
CHUNK = 4096
VMEM = pl.BlockSpec(memory_space=pltpu.VMEM)
SMEM = pl.BlockSpec(memory_space=pltpu.SMEM)
HBM = pl.BlockSpec(memory_space=pltpu.HBM)


def call(kernel, out_shape, in_specs, scratch=(), limit=4):
    many = isinstance(out_shape, (tuple, list))
    inner = pl.pallas_call(
        kernel,
        out_shape=out_shape,
        in_specs=in_specs,
        out_specs=[VMEM] * len(out_shape) if many else VMEM,
        scratch_shapes=list(scratch),
        compiler_params=pltpu.CompilerParams(vmem_limit_bytes=limit << 20),
    )

    def run(*args):
        return inner(
            *(pltpu.with_memory_space_constraint(x, pltpu.HBM) if s is HBM else x for x, s in zip(args, in_specs))
        )

    return run


def dot(a, b):
    return jnp.dot(a, b, preferred_element_type=F32)


def dot_t(a, b):
    return lax.dot_general(a, b, (((1,), (1,)), ((), ())), preferred_element_type=F32)


def split2(x):
    high = x.astype(BF16)
    return high, (x - high.astype(F32)).astype(BF16)


def lane_split(square):
    high, low = split2(square)
    lane = lax.broadcasted_iota(jnp.int32, square.shape, 1)
    return jnp.where(lane < LANES // 2, high.astype(F32), low.astype(F32)).astype(BF16)


def lane_join(pair):
    return pair + pltpu.roll(pair, LANES // 2, 1)


def core_index():
    return lax.rem(lax.axis_index("seq"), 2)


def project_kernel(
    resid,
    gain,
    w_query,
    w_key,
    w_value,
    angle,
    keep,
    send,
    cos,
    sin,
    x_buf,
    gain_buf,
    q_buf,
    kv_buf,
    angle_buf,
    sems,
):
    mine = core_index()
    pairs = [
        (angle, angle_buf),
        (resid, x_buf),
        (gain, gain_buf),
        (w_key, kv_buf.at[0]),
        (w_value, kv_buf.at[1]),
        (w_query, q_buf),
    ]
    loads = [pltpu.make_async_copy(src, dst, sems.at[i]) for i, (src, dst) in enumerate(pairs)]
    for load in loads:
        load.start()
    loads[0].wait()
    cosine, sine = jnp.cos(angle_buf[...]), jnp.sin(angle_buf[...])
    cos[...] = jnp.concatenate([cosine, cosine], axis=1)
    sin[...] = jnp.concatenate([-sine, sine], axis=1)
    loads[1].wait()
    loads[2].wait()
    x32 = x_buf[...].astype(F32)
    x = (x32 * gain_buf[...].astype(F32)[None, :]).astype(BF16)
    square = jnp.broadcast_to(jnp.sum(x32 * x32, axis=1, keepdims=True), (32, LANES))
    for load in loads[3:]:
        load.wait()
    for target, half in ((keep, mine), (send, 1 - mine)):
        cols = pl.ds(pl.multiple_of(half * 512, LANES), 512)
        target[:, 0:512] = dot(x, q_buf[:, cols])
        target[:, 512:640] = dot(x, kv_buf[half])
        target[:, 640:768] = square


def project_pair_kernel(own, other, copies):
    total = own[...] + other[...]
    row_log = jnp.log2(total[:, 640:768] + TINY)
    meta = [jnp.floor(row_log * 256 + 0.5)]
    meta.append(jnp.floor((row_log * 256 - meta[0]) * 16384 + 0.5))
    coded = []
    for cols in (slice(0, 512), slice(512, 640)):
        x = total[:, cols]
        grade = jnp.ceil(jnp.log2(jnp.max(jnp.abs(x), axis=1, keepdims=True) + TINY))
        coded.append(jnp.floor(x * (FULL * jnp.exp2(-grade)) + 0.5))
        meta.append(jnp.broadcast_to(grade, (32, LANES)))
    lane = lax.broadcasted_iota(jnp.int32, (32, LANES), 1)
    last = jnp.where(lane < 2, jnp.where(lane == 0, meta[0], meta[1]), jnp.where(lane == 2, meta[2], meta[3]))
    sent = jnp.concatenate(coded + [last], axis=1).astype(jnp.int32).astype(jnp.int16)
    for j in range(8):
        copies[j] = sent


def rotate_kernel(parts, cos, sin, out):
    total = jnp.zeros((32, 640), F32)
    square = jnp.zeros((32, 1), F32)
    for j in range(8):
        part = parts[j].astype(jnp.int32).astype(F32)
        meta = part[:, 640:768]
        square += jnp.exp2(meta[:, 0:1] / 256 + meta[:, 1:2] / (256 * 16384))
        step = jnp.exp2(meta) / FULL
        total += jnp.concatenate([part[:, 0:512] * step[:, 2:3], part[:, 512:640] * step[:, 3:4]], axis=1)
    total = total * lax.rsqrt(square / 8192 + EPS)
    turned = []
    for g in range(5):
        x = total[:, g * 128 : (g + 1) * 128]
        turned.append(x * cos[...] + pltpu.roll(x, LANES // 2, 1) * sin[...])
    last = jnp.where(core_index() == 0, turned[4], total[:, 512:640])
    for g, x in enumerate(turned[:4] + [last]):
        out[g * 32 : (g + 1) * 32, :] = x.astype(BF16)


def fold(x, op):
    out = x[:, 0:LANES]
    for i in range(1, x.shape[1] // LANES):
        out = op(out, x[:, i * LANES : (i + 1) * LANES])
    return out


def attend_kernel(
    own, other, positions, valid, keys, values, keep, send, query, scores, acc, o_acc, v_buf, v_sem
):
    scale = 128.0**-0.5
    power = scale * 1.4426950408889634
    mine = core_index()
    length = valid[0]
    whole = lax.div(length, CHUNK)
    used = lax.div(length + (CHUNK - 1), CHUNK)

    def load(c):
        rows = pl.ds(pl.multiple_of(c * CHUNK, CHUNK), CHUNK)
        return pltpu.make_async_copy(values.at[0, rows, :], v_buf.at[rows, :], v_sem.at[c])

    @pl.loop(0, used)
    def _(c):
        load(c).start()

    row = lax.broadcasted_iota(jnp.int32, (32, LANES), 0)
    lane = lax.broadcasted_iota(jnp.int32, (32, LANES), 1)
    of_row = jnp.zeros((32, LANES), jnp.int32)
    of_lane = jnp.full((32, LANES), 1 << 20, jnp.int32)
    for i in range(32):
        of_row = jnp.where(row == i, positions[i], of_row)
        of_lane = jnp.where(lane == i, positions[i], of_lane)
    allowed = (of_lane <= of_row) & (lax.axis_index("seq") == 0)
    query[pl.ds(pl.multiple_of(mine * 128, 128), 128), :] = own[0:128, :]
    query[pl.ds(pl.multiple_of((1 - mine) * 128, 128), 128), :] = other[0:128, :]
    q = query[...]
    pad = jnp.zeros((96, LANES), BF16)
    a, b = own[128:160, :].astype(F32), other[128:160, :].astype(F32)
    k_new = jnp.concatenate([jnp.where(mine == 0, a, b).astype(BF16), pad], axis=0)
    v_new = jnp.concatenate([jnp.where(mine == 0, b, a).astype(BF16), pad], axis=0)

    def score(c):
        rows = pl.ds(pl.multiple_of(c * CHUNK, CHUNK), CHUNK)
        return dot_t(q, keys[0, rows, :])

    acc[...] = jnp.full((256, LANES), LOW, F32)

    @pl.loop(0, whole)
    def _(c):
        s = score(c)
        scores[c] = s
        acc[...] = jnp.maximum(acc[...], fold(s, jnp.maximum))

    @pl.when(used > whole)
    def _():
        slot = lax.broadcasted_iota(jnp.int32, (256, CHUNK), 1) + whole * CHUNK
        s = jnp.where(slot < length, score(whole), LOW)
        scores[whole] = s
        acc[...] = jnp.maximum(acc[...], fold(s, jnp.maximum))

    top = jnp.max(acc[...], axis=1, keepdims=True)
    shift = top * power
    acc[...] = jnp.zeros((256, LANES), F32)
    o_acc[...] = jnp.zeros((256, LANES), F32)

    @pl.loop(0, used)
    def _(c):
        rows = pl.ds(pl.multiple_of(c * CHUNK, CHUNK), CHUNK)
        e = jnp.exp2(scores[c] * power - shift).astype(BF16)
        acc[...] += fold(e.astype(F32), jnp.add)
        load(c).wait()
        o_acc[...] += dot(e, v_buf[rows, :])

    total_l = jnp.sum(acc[...], axis=1, keepdims=True)
    lse = top * scale + jnp.log(total_l)
    summed = o_acc[...] / total_l

    hold = jnp.concatenate([jnp.where(allowed, 0.0, -1.0)] * 8, axis=0)
    s_new = jnp.where(hold < 0, LOW, dot_t(q, k_new) * scale)
    top_new = jnp.max(s_new, axis=1, keepdims=True)
    e_new = jnp.exp(s_new - top_new).astype(BF16)
    l_new = jnp.sum(e_new.astype(F32), axis=1, keepdims=True)
    o_new = dot(e_new, v_new) / l_new
    lse_new = top_new + jnp.log(l_new)

    high = jnp.maximum(lse, lse_new)
    f_old = jnp.exp(lse - high)
    f_new = jnp.exp(lse_new - high)
    both = f_old + f_new
    o_acc[...] = (summed * f_old + o_new * f_new) / both
    acc[...] = jnp.broadcast_to(high + jnp.log(both), (256, LANES))
    for target, half in ((keep, mine), (send, 1 - mine)):
        rows = pl.ds(pl.multiple_of(half * 128, 128), 128)
        target[0:128, :] = o_acc[rows, :]
        target[128:256, :] = acc[rows, :]


def merge_pair_kernel(own, other, copies):
    la, lb = own[128:256, :], other[128:256, :]
    high = jnp.maximum(la, lb)
    fa, fb = jnp.exp(la - high), jnp.exp(lb - high)
    both = fa + fb
    o = ((own[0:128, :] * fa + other[0:128, :] * fb) / both).astype(BF16)
    lanes = jnp.transpose(high + jnp.log(both))[0:8]
    row = lax.broadcasted_iota(jnp.int32, (8, LANES), 0)
    p0 = lanes.astype(BF16).astype(F32)
    rest = lanes - p0
    p1 = rest.astype(BF16).astype(F32)
    p2 = rest - p1
    tail = jnp.where(row == 0, p0, jnp.where(row == 1, p1, p2))
    tail = jnp.concatenate([tail, jnp.zeros((8, LANES), F32)], axis=0).astype(BF16)
    for j in range(8):
        copies[j, 0:128, :] = o
        copies[j, 128:144, :] = tail


def merge_kernel(parts, attn):
    rows = []
    for j in range(8):
        tail = parts[j, 128:144, :].astype(F32)
        rows.append(tail[0:1] + tail[1:2] + tail[2:3])
    lse = jnp.concatenate(rows, axis=0)
    weight = jnp.exp(lse - jnp.max(lse, axis=0, keepdims=True))
    weight = weight / jnp.sum(weight, axis=0, keepdims=True)
    weight = jnp.transpose(jnp.concatenate([weight, jnp.zeros((120, LANES), F32)], axis=0))
    total = parts[0, 0:128, :].astype(F32) * weight[:, 0:1]
    for j in range(1, 8):
        total += parts[j, 0:128, :].astype(F32) * weight[:, j : j + 1]
    for g in range(4):
        attn[:, g * 128 : (g + 1) * 128] = total[g * 32 : (g + 1) * 32].astype(BF16)


def out_kernel(own, other, w_out, copies):
    mine = core_index()
    total = jnp.zeros((32, 512), F32)
    for source, half in ((own, mine), (other, 1 - mine)):
        total += dot(source[...], w_out[pl.ds(pl.multiple_of(half * 512, LANES), 512), :])
    part = total.astype(BF16)
    for j in range(8):
        copies[j] = part


def sum_parts(parts):
    total = parts[0].astype(F32)
    for j in range(1, 8):
        total = total + parts[j].astype(F32)
    return total


def gate_up_kernel(parts, resid, gain, w_gate, w_up, attn_out, mid, keep, send):
    branch = sum_parts(parts).astype(BF16)
    attn_out[...] = branch
    hidden = (resid[...].astype(F32) + branch.astype(F32)).astype(BF16)
    mid[...] = hidden
    x32 = hidden.astype(F32)
    x = (x32 * gain[...].astype(F32)[None, :]).astype(BF16)
    square = jnp.broadcast_to(jnp.sum(x32 * x32, axis=1, keepdims=True), (32, LANES))
    mine = core_index()
    for target, half in ((keep, mine), (send, 1 - mine)):
        for i in range(2):
            cols = pl.ds(pl.multiple_of(half * 1792 + i * 896, LANES), 896)
            target[:, i * 896 : (i + 1) * 896] = dot(x, w_gate[:, cols]).astype(target.dtype)
            target[:, 1792 + i * 896 : 1792 + (i + 1) * 896] = dot(x, w_up[:, cols]).astype(target.dtype)
    keep[:, 3584:3712] = square
    send[:, 3584:3712] = lane_split(square)


def gate_up_pair_kernel(keep, got, pieces):
    square = keep[:, 3584:3712] + lane_join(got[:, 3584:3712].astype(F32))
    high = square.astype(BF16).astype(F32)
    low = square - high
    for j in range(8):
        rows = slice((j // 2) * 8, (j // 2) * 8 + 8)
        block = []
        for base in (0, 1792):
            cols = slice(base + (j % 2) * 896, base + (j % 2 + 1) * 896)
            block.append(keep[rows, cols] + got[:, cols].astype(F32)[rows])
        pieces[j, :, 0:896] = jnp.concatenate(block, axis=0).astype(BF16)
        pieces[j, :, 896:1024] = jnp.concatenate([high[rows], low[rows]], axis=0).astype(BF16)


def act_kernel(parts, copies):
    total = sum_parts(parts)
    square = (total[0:8] + total[8:16])[:, 896:897]
    inv = lax.rsqrt(square / 8192 + EPS)
    gate = total[0:8, 0:896] * inv
    up = total[8:16, 0:896] * inv
    act = gate / (1.0 + jnp.exp(-gate)) * up
    packed = jnp.concatenate(
        [act[:, 0:512], jnp.concatenate([act[:, 512:896], jnp.zeros((8, LANES), F32)], axis=1)], axis=0
    ).astype(BF16)
    for j in range(8):
        copies[j] = packed


def down_kernel(own, other, w_down, copies):
    total = jnp.zeros((32, 512), F32)
    mine = core_index()
    for source, half in ((own, mine), (other, 1 - mine)):
        for ch in range(2):
            wide = []
            for rg in range(4):
                piece = source[rg * 2 + ch].astype(F32)
                wide.append(jnp.concatenate([piece[0:8], piece[8:16, 0:384]], axis=1))
            act = jnp.concatenate(wide, axis=0).astype(BF16)
            rows = pl.ds(pl.multiple_of(half * 1792 + ch * 896, LANES), 896)
            total += dot(act, w_down[rows, :])
    part = total.astype(BF16)
    for j in range(8):
        copies[j] = part


def final_kernel(parts, mid, layer_out):
    layer_out[...] = (mid[...].astype(F32) + sum_parts(parts)).astype(BF16)


def body(
    resid,
    attn_gain,
    ffn_gain,
    w_query,
    w_key,
    w_value,
    w_out,
    rope_angle,
    positions,
    cache_keys,
    cache_values,
    valid_lengths,
    w_gate,
    w_up,
    w_down,
):
    shape = jax.ShapeDtypeStruct
    near = pltpu.VMEM
    same_core = [[2 * j + c for j in range(8)] for c in range(2)]
    swap = [(i, i ^ 1) for i in range(16)]

    def to_other_core(x):
        return lax.ppermute(x, "seq", swap)

    def over_chips(x):
        return lax.all_to_all(x, "seq", 0, 0, axis_index_groups=same_core)

    def over_tp(x):
        return lax.all_to_all(x, "tp", 0, 0)

    table = near((32, LANES), F32)
    keep, send, cos, sin = call(
        project_kernel,
        (near((32, 768), F32), near((32, 768), F32), table, table),
        [HBM] * 6,
        scratch=[
            pltpu.VMEM((32, 512), BF16),
            pltpu.VMEM((512,), BF16),
            pltpu.VMEM((512, 1024), BF16),
            pltpu.VMEM((2, 512, LANES), BF16),
            pltpu.VMEM((32, 64), F32),
            pltpu.SemaphoreType.DMA((6,)),
        ],
    )(resid, attn_gain, w_query, w_key, w_value, rope_angle)
    copies = call(project_pair_kernel, near((8, 32, 768), jnp.int16), [VMEM] * 2)(keep, to_other_core(send))
    turned = call(rotate_kernel, near((160, LANES), BF16), [VMEM] * 3)(over_chips(copies), cos, sin)

    chunks = 16384 // CHUNK
    keep, send = call(
        attend_kernel,
        (near((256, LANES), F32), near((256, LANES), F32)),
        [VMEM] * 2 + [SMEM] * 2 + [VMEM, HBM],
        scratch=[
            pltpu.VMEM((256, LANES), BF16),
            pltpu.VMEM((chunks, 256, CHUNK), F32),
            pltpu.VMEM((256, LANES), F32),
            pltpu.VMEM((256, LANES), F32),
            pltpu.VMEM((16384, LANES), BF16),
            pltpu.SemaphoreType.DMA((chunks,)),
        ],
        limit=30,
    )(turned, to_other_core(turned), positions, valid_lengths, cache_keys, cache_values)
    copies = call(merge_pair_kernel, near((8, 144, LANES), BF16), [VMEM] * 2)(keep, to_other_core(send))
    attn = call(merge_kernel, near((32, 512), BF16), [VMEM])(over_chips(copies))
    copies = call(out_kernel, near((8, 32, 512), BF16), [VMEM] * 3)(attn, to_other_core(attn), w_out)
    parts = over_tp(copies)

    attn_out, mid, keep, send = call(
        gate_up_kernel,
        (shape((32, 512), BF16), near((32, 512), BF16), near((32, 3712), F32), near((32, 3712), BF16)),
        [VMEM] * 5,
        limit=12,
    )(parts, resid, ffn_gain, w_gate, w_up)
    pieces = call(gate_up_pair_kernel, near((8, 16, 1024), BF16), [VMEM] * 2)(keep, to_other_core(send))
    parts = over_chips(pieces)
    copies = call(act_kernel, near((8, 16, 512), BF16), [VMEM])(parts)
    acts = over_chips(copies)
    copies = call(down_kernel, near((8, 32, 512), BF16), [VMEM] * 3, limit=8)(acts, to_other_core(acts), w_down)
    parts = over_tp(copies)
    layer_out = call(final_kernel, shape((32, 512), BF16), [VMEM] * 2)(parts, mid)
    return (attn_out, layer_out)


def solution(mesh):
    in_specs = (
        P(None, "seq"),
        P("seq"),
        P("seq"),
        P("seq", "tp"),
        P("seq", "tp"),
        P("seq", "tp"),
        P("tp", "seq"),
        P(),
        P(),
        P("tp", "seq", None),
        P("tp", "seq", None),
        P("seq"),
        P("seq", "tp"),
        P("seq", "tp"),
        P("tp", "seq"),
    )
    out_specs = (P(None, "seq"), P(None, "seq"))
    return jax.shard_map(body, mesh=mesh, in_specs=in_specs, out_specs=out_specs, check_vma=False)
```

```python
import functools
import math

import jax
import jax.numpy as jnp
from jax import lax
from jax.experimental import pallas as pl
from jax.experimental.pallas import tpu as pltpu
from jax.sharding import PartitionSpec as P

EPS = 1e-05
LOW = -1e30
TINY = 1e-30
FULL = 32766.0
F32 = jnp.float32
BF16 = jnp.bfloat16
LANES = 128
CHUNK = 8192
PIECE = 1024
VMEM = pl.BlockSpec(memory_space=pltpu.VMEM)
SMEM = pl.BlockSpec(memory_space=pltpu.SMEM)
HBM = pl.BlockSpec(memory_space=pltpu.HBM)


def call(kernel, out_shape, in_specs, scratch=(), limit=4, moved=0):
    many = isinstance(out_shape, (tuple, list))
    inner = pl.pallas_call(
        kernel,
        out_shape=out_shape,
        in_specs=in_specs,
        out_specs=[VMEM] * len(out_shape) if many else VMEM,
        scratch_shapes=list(scratch),
        compiler_params=pltpu.CompilerParams(vmem_limit_bytes=limit << 20),
        cost_estimate=pl.CostEstimate(flops=0, bytes_accessed=moved, transcendentals=0) if moved else None,
    )

    def run(*args):
        return inner(
            *(pltpu.with_memory_space_constraint(x, pltpu.HBM) if s is HBM else x for x, s in zip(args, in_specs))
        )

    return run


def dot(a, b):
    return jnp.dot(a, b, preferred_element_type=F32)


def dot_t(a, b):
    return lax.dot_general(a, b, (((1,), (1,)), ((), ())), preferred_element_type=F32)


def dot_tt(a, b):
    return lax.dot_general(a, b, (((0,), (0,)), ((), ())), preferred_element_type=F32)


def split2(x):
    high = x.astype(BF16)
    return high, (x - high.astype(F32)).astype(BF16)


def lane_split(square):
    high, low = split2(square)
    lane = lax.broadcasted_iota(jnp.int32, square.shape, 1)
    return jnp.where(lane < LANES // 2, high.astype(F32), low.astype(F32)).astype(BF16)


def lane_join(pair):
    return pair + pltpu.roll(pair, LANES // 2, 1)


def core_index():
    return lax.rem(lax.axis_index("seq"), 2)


def project_kernel(
    resid,
    gain,
    w_query,
    w_key,
    w_value,
    angle,
    keep,
    send,
    cos,
    sin,
    x_buf,
    gain_buf,
    q_buf,
    kv_buf,
    angle_buf,
    sems,
):
    mine = core_index()
    pairs = [
        (angle, angle_buf),
        (resid, x_buf),
        (gain, gain_buf),
        (w_key, kv_buf.at[0]),
        (w_value, kv_buf.at[1]),
        (w_query, q_buf),
    ]
    loads = [pltpu.make_async_copy(src, dst, sems.at[i]) for i, (src, dst) in enumerate(pairs)]
    for load in loads:
        load.start()
    loads[0].wait()
    cosine, sine = jnp.cos(angle_buf[...]), jnp.sin(angle_buf[...])
    cos[...] = jnp.concatenate([cosine, cosine], axis=1)
    sin[...] = jnp.concatenate([-sine, sine], axis=1)
    loads[1].wait()
    loads[2].wait()
    x32 = x_buf[...].astype(F32)
    x = (x32 * gain_buf[...].astype(F32)[None, :]).astype(BF16)
    square = jnp.broadcast_to(jnp.sum(x32 * x32, axis=1, keepdims=True), (32, LANES))
    for load in loads[3:]:
        load.wait()
    for target, half in ((keep, mine), (send, 1 - mine)):
        cols = pl.ds(pl.multiple_of(half * 512, LANES), 512)
        target[:, 0:512] = dot(x, q_buf[:, cols])
        target[:, 512:640] = dot(x, kv_buf[half])
        target[:, 640:768] = square


def project_pair_kernel(own, other, w1, w2, w3, copies):
    total = own[...] + other[...]
    row_log = jnp.log2(total[:, 640:768] + TINY)
    meta = [jnp.floor(row_log * 256 + 0.5)]
    meta.append(jnp.floor((row_log * 256 - meta[0]) * 16384 + 0.5))
    coded = []
    for cols in (slice(0, 512), slice(512, 640)):
        x = total[:, cols]
        grade = jnp.ceil(jnp.log2(jnp.max(jnp.abs(x), axis=1, keepdims=True) + TINY))
        coded.append(jnp.floor(x * (FULL * jnp.exp2(-grade)) + 0.5))
        meta.append(jnp.broadcast_to(grade, (32, LANES)))
    lane = lax.broadcasted_iota(jnp.int32, (32, LANES), 1)
    last = jnp.where(lane < 2, jnp.where(lane == 0, meta[0], meta[1]), jnp.where(lane == 2, meta[2], meta[3]))
    sent = jnp.concatenate(coded + [last], axis=1).astype(jnp.int32).astype(jnp.int16)
    for j in range(8):
        copies[j] = sent


def rotate_kernel(parts, cos, sin, out):
    total = jnp.zeros((32, 640), F32)
    square = jnp.zeros((32, 1), F32)
    for j in range(8):
        part = parts[j].astype(jnp.int32).astype(F32)
        meta = part[:, 640:768]
        square += jnp.exp2(meta[:, 0:1] / 256 + meta[:, 1:2] / (256 * 16384))
        step = jnp.exp2(meta) / FULL
        total += jnp.concatenate([part[:, 0:512] * step[:, 2:3], part[:, 512:640] * step[:, 3:4]], axis=1)
    total = total * lax.rsqrt(square / 8192 + EPS)
    turned = []
    for g in range(5):
        x = total[:, g * 128 : (g + 1) * 128]
        turned.append(x * cos[...] + pltpu.roll(x, LANES // 2, 1) * sin[...])
    last = jnp.where(core_index() == 0, turned[4], total[:, 512:640])
    for g, x in enumerate(turned[:4] + [last]):
        out[g * 32 : (g + 1) * 32, :] = x.astype(BF16)


def attend_kernel(own, other, positions, valid, keys, values, keep, send, query, shift, total_l, total_o):
    scale = 128.0**-0.5
    power = scale * 1.4426950408889634
    mine = core_index()
    length = valid[0]

    query[pl.ds(pl.multiple_of(mine * 128, 128), 128), :] = own[0:128, :]
    query[pl.ds(pl.multiple_of((1 - mine) * 128, 128), 128), :] = other[0:128, :]
    q = query[...]
    a, b = own[128:160, :].astype(F32), other[128:160, :].astype(F32)
    k_new = jnp.where(mine == 0, a, b).astype(BF16)
    v_new = jnp.where(mine == 0, b, a).astype(BF16)

    def score(start):
        return dot_t(keys[0, pl.ds(start, PIECE), :], q)

    def only_valid(s, start):
        slot = lax.broadcasted_iota(jnp.int32, (PIECE, 256), 0) + start
        return jnp.where(slot < length, s, LOW)

    def weigh(s, start, carry):
        sums, o = carry
        e = jnp.exp2(s * power - shift[0:1, :]).astype(BF16)
        sums = sums + jnp.sum(e.astype(F32).reshape(PIECE // 8, 8, 256), axis=0)
        return sums, o + dot_tt(values[0, pl.ds(start, PIECE), :], e)

    def run(first, pieces, masked):
        carry = (total_l[...], total_o[...])
        starts = [pl.multiple_of(first + i * PIECE, PIECE) for i in range(pieces)]
        s = score(starts[0])
        for i in range(pieces):
            ahead = score(starts[i + 1]) if i + 1 < pieces else None
            carry = weigh(only_valid(s, starts[i]) if masked else s, starts[i], carry)
            s = ahead
        total_l[...], total_o[...] = carry

    def restart(top):
        shift[...] = jnp.broadcast_to(top * power, (8, 256))
        total_l[...] = jnp.zeros((8, 256), F32)
        total_o[...] = jnp.zeros((LANES, 256), F32)

    restart(jnp.max(only_valid(score(0), 0), axis=0, keepdims=True))
    whole = lax.div(length, CHUNK)

    @pl.loop(0, whole)
    def _(c):
        run(pl.multiple_of(c * CHUNK, CHUNK), CHUNK // PIECE, False)

    @pl.when(whole * CHUNK < length)
    def _():
        run(pl.multiple_of(whole * CHUNK, CHUNK), CHUNK // PIECE, True)

    @pl.when(jnp.logical_not(jnp.max(total_l[...]) < 1e30))
    def _():
        pieces = lax.div(length + (PIECE - 1), PIECE)
        shift[...] = jnp.full((8, 256), LOW, F32)

        @pl.loop(0, pieces)
        def _(c):
            start = pl.multiple_of(c * PIECE, PIECE)
            top = jnp.max(only_valid(score(start), start), axis=0, keepdims=True)
            shift[...] = jnp.maximum(shift[...], top)

        restart(shift[0:1, :])

        @pl.loop(0, pieces)
        def _(c):
            run(pl.multiple_of(c * PIECE, PIECE), 1, True)

    l_old = jnp.sum(total_l[...], axis=0, keepdims=True)
    lse_old = shift[0:1, :] * math.log(2.0) + jnp.log(l_old)

    lane = lax.broadcasted_iota(jnp.int32, (8, 256), 1) & 31
    row = lax.broadcasted_iota(jnp.int32, (32, LANES), 0)
    of_query = jnp.zeros((8, 256), jnp.int32)
    of_key = jnp.zeros((32, LANES), jnp.int32)
    for i in range(32):
        of_query = jnp.where(lane == i, positions[i], of_query)
        of_key = jnp.where(row == i, positions[i], of_key)
    of_key = jnp.concatenate([of_key, of_key], axis=1)
    allowed = (of_key <= of_query[0:1, :]) & (lax.axis_index("seq") == 0)
    s_new = jnp.where(allowed, dot_t(k_new, q) * scale, LOW)
    top_new = jnp.max(s_new, axis=0, keepdims=True)
    e_new = jnp.exp(s_new - top_new).astype(BF16)
    l_new = jnp.sum(e_new.astype(F32), axis=0, keepdims=True)
    lse_new = top_new + jnp.log(l_new)
    o_new = dot_tt(v_new, e_new)

    high = jnp.maximum(lse_old, lse_new)
    f_old = jnp.exp(lse_old - high)
    f_new = jnp.exp(lse_new - high)
    both = f_old + f_new
    o = total_o[...] * (f_old / (l_old * both)) + o_new * (f_new / (l_new * both))
    lse = jnp.broadcast_to(high + jnp.log(both), (8, 256))
    for target, first in ((keep, mine == 0), (send, mine != 0)):
        target[0:128, :] = jnp.where(first, o[:, 0:128], o[:, 128:256])
        target[128:136, :] = jnp.where(first, lse[:, 0:128], lse[:, 128:256])


def merge_pair_kernel(own, other, copies):
    la, lb = own[128:136, :], other[128:136, :]
    high = jnp.maximum(la, lb)
    fa, fb = jnp.exp(la - high), jnp.exp(lb - high)
    both = fa + fb
    o = (own[0:128, :] * (fa / both)[0:1] + other[0:128, :] * (fb / both)[0:1]).astype(BF16)
    lse = high + jnp.log(both)
    p0 = lse.astype(BF16).astype(F32)
    rest = lse - p0
    p1 = rest.astype(BF16).astype(F32)
    p2 = rest - p1
    row = lax.broadcasted_iota(jnp.int32, (8, LANES), 0)
    tail = jnp.where(row == 0, p0, jnp.where(row == 1, p1, p2))
    tail = jnp.concatenate([tail, jnp.zeros((8, LANES), F32)], axis=0).astype(BF16)
    for j in range(8):
        copies[j, 0:128, :] = o
        copies[j, 128:144, :] = tail


def merge_kernel(parts, attn):
    rows = []
    for j in range(8):
        tail = parts[j, 128:144, :].astype(F32)
        rows.append(tail[0:1] + tail[1:2] + tail[2:3])
    high = functools.reduce(jnp.maximum, rows)
    weights = [jnp.exp(r - high) for r in rows]
    both = functools.reduce(jnp.add, weights)
    total = parts[0, 0:128, :].astype(F32) * (weights[0] / both)
    for j in range(1, 8):
        total += parts[j, 0:128, :].astype(F32) * (weights[j] / both)
    total = jnp.transpose(total)
    for g in range(4):
        attn[:, g * 128 : (g + 1) * 128] = total[g * 32 : (g + 1) * 32].astype(BF16)


def out_kernel(own, other, w_out, copies):
    mine = core_index()
    total = jnp.zeros((32, 512), F32)
    for source, half in ((own, mine), (other, 1 - mine)):
        total += dot(source[...], w_out[pl.ds(pl.multiple_of(half * 512, LANES), 512), :])
    part = total.astype(BF16)
    for j in range(8):
        copies[j] = part


def sum_parts(parts):
    total = parts[0].astype(F32)
    for j in range(1, 8):
        total = total + parts[j].astype(F32)
    return total


def gate_up_kernel(parts, resid, gain, w_gate, w_up, attn_out, mid, keep, send):
    branch = sum_parts(parts).astype(BF16)
    attn_out[...] = branch
    hidden = (resid[...].astype(F32) + branch.astype(F32)).astype(BF16)
    mid[...] = hidden
    x32 = hidden.astype(F32)
    x = (x32 * gain[...].astype(F32)[None, :]).astype(BF16)
    square = jnp.broadcast_to(jnp.sum(x32 * x32, axis=1, keepdims=True), (32, LANES))
    mine = core_index()
    for target, half in ((keep, mine), (send, 1 - mine)):
        for i in range(2):
            cols = pl.ds(pl.multiple_of(half * 1792 + i * 896, LANES), 896)
            target[:, i * 896 : (i + 1) * 896] = dot(x, w_gate[:, cols]).astype(target.dtype)
            target[:, 1792 + i * 896 : 1792 + (i + 1) * 896] = dot(x, w_up[:, cols]).astype(target.dtype)
    keep[:, 3584:3712] = square
    send[:, 3584:3712] = lane_split(square)


def gate_up_pair_kernel(keep, got, pieces):
    square = keep[:, 3584:3712] + lane_join(got[:, 3584:3712].astype(F32))
    high = square.astype(BF16).astype(F32)
    low = square - high
    for j in range(8):
        rows = slice((j // 2) * 8, (j // 2) * 8 + 8)
        block = []
        for base in (0, 1792):
            cols = slice(base + (j % 2) * 896, base + (j % 2 + 1) * 896)
            block.append(keep[rows, cols] + got[:, cols].astype(F32)[rows])
        pieces[j, :, 0:896] = jnp.concatenate(block, axis=0).astype(BF16)
        pieces[j, :, 896:1024] = jnp.concatenate([high[rows], low[rows]], axis=0).astype(BF16)


def act_kernel(parts, copies):
    total = sum_parts(parts)
    square = (total[0:8] + total[8:16])[:, 896:897]
    inv = lax.rsqrt(square / 8192 + EPS)
    gate = total[0:8, 0:896] * inv
    up = total[8:16, 0:896] * inv
    act = gate / (1.0 + jnp.exp(-gate)) * up
    packed = jnp.concatenate(
        [act[:, 0:512], jnp.concatenate([act[:, 512:896], jnp.zeros((8, LANES), F32)], axis=1)], axis=0
    ).astype(BF16)
    for j in range(8):
        copies[j] = packed


def down_kernel(own, other, w_down, copies):
    total = jnp.zeros((32, 512), F32)
    mine = core_index()
    for source, half in ((own, mine), (other, 1 - mine)):
        for ch in range(2):
            wide = []
            for rg in range(4):
                piece = source[rg * 2 + ch].astype(F32)
                wide.append(jnp.concatenate([piece[0:8], piece[8:16, 0:384]], axis=1))
            act = jnp.concatenate(wide, axis=0).astype(BF16)
            rows = pl.ds(pl.multiple_of(half * 1792 + ch * 896, LANES), 896)
            total += dot(act, w_down[rows, :])
    part = total.astype(BF16)
    for j in range(8):
        copies[j] = part


def final_kernel(parts, mid, layer_out):
    layer_out[...] = (mid[...].astype(F32) + sum_parts(parts)).astype(BF16)


def body(
    resid,
    attn_gain,
    ffn_gain,
    w_query,
    w_key,
    w_value,
    w_out,
    rope_angle,
    positions,
    cache_keys,
    cache_values,
    valid_lengths,
    w_gate,
    w_up,
    w_down,
):
    shape = jax.ShapeDtypeStruct
    near = pltpu.VMEM
    same_core = [[2 * j + c for j in range(8)] for c in range(2)]
    swap = [(i, i ^ 1) for i in range(16)]

    def to_other_core(x):
        return lax.ppermute(x, "seq", swap)

    def over_chips(x):
        return lax.all_to_all(x, "seq", 0, 0, axis_index_groups=same_core)

    def over_tp(x):
        return lax.all_to_all(x, "tp", 0, 0)

    table = near((32, LANES), F32)
    keep, send, cos, sin = call(
        project_kernel,
        (near((32, 768), F32), near((32, 768), F32), table, table),
        [HBM] * 6,
        scratch=[
            pltpu.VMEM((32, 512), BF16),
            pltpu.VMEM((512,), BF16),
            pltpu.VMEM((512, 1024), BF16),
            pltpu.VMEM((2, 512, LANES), BF16),
            pltpu.VMEM((32, 64), F32),
            pltpu.SemaphoreType.DMA((6,)),
        ],
    )(resid, attn_gain, w_query, w_key, w_value, rope_angle)
    copies = call(project_pair_kernel, near((8, 32, 768), jnp.int16), [VMEM] * 2 + [HBM] * 3)(
        keep, to_other_core(send), w_gate, w_up, w_down
    )
    turned = call(rotate_kernel, near((160, LANES), BF16), [VMEM] * 3)(over_chips(copies), cos, sin)

    keep, send = call(
        attend_kernel,
        (near((136, LANES), F32), near((136, LANES), F32)),
        [VMEM] * 2 + [SMEM] * 2 + [VMEM] * 2,
        scratch=[
            pltpu.VMEM((256, LANES), BF16),
            pltpu.VMEM((8, 256), F32),
            pltpu.VMEM((8, 256), F32),
            pltpu.VMEM((LANES, 256), F32),
        ],
        limit=24,
    )(turned, to_other_core(turned), positions, valid_lengths, cache_keys, cache_values)
    copies = call(merge_pair_kernel, near((8, 144, LANES), BF16), [VMEM] * 2)(keep, to_other_core(send))
    attn = call(merge_kernel, near((32, 512), BF16), [VMEM])(over_chips(copies))
    copies = call(out_kernel, near((8, 32, 512), BF16), [VMEM] * 3)(attn, to_other_core(attn), w_out)
    parts = over_tp(copies)

    attn_out, mid, keep, send = call(
        gate_up_kernel,
        (shape((32, 512), BF16), near((32, 512), BF16), near((32, 3712), F32), near((32, 3712), BF16)),
        [VMEM] * 5,
        limit=12,
    )(parts, resid, ffn_gain, w_gate, w_up)
    pieces = call(gate_up_pair_kernel, near((8, 16, 1024), BF16), [VMEM] * 2)(keep, to_other_core(send))
    parts = over_chips(pieces)
    copies = call(act_kernel, near((8, 16, 512), BF16), [VMEM])(parts)
    acts = over_chips(copies)
    copies = call(down_kernel, near((8, 32, 512), BF16), [VMEM] * 3, limit=8)(acts, to_other_core(acts), w_down)
    parts = over_tp(copies)
    layer_out = call(final_kernel, shape((32, 512), BF16), [VMEM] * 2)(parts, mid)
    return (attn_out, layer_out)


def solution(mesh):
    in_specs = (
        P(None, "seq"),
        P("seq"),
        P("seq"),
        P("seq", "tp"),
        P("seq", "tp"),
        P("seq", "tp"),
        P("tp", "seq"),
        P(),
        P(),
        P("tp", "seq", None),
        P("tp", "seq", None),
        P("seq"),
        P("seq", "tp"),
        P("seq", "tp"),
        P("tp", "seq"),
    )
    out_specs = (P(None, "seq"), P(None, "seq"))
    return jax.shard_map(body, mesh=mesh, in_specs=in_specs, out_specs=out_specs, check_vma=False)
```

```python
import functools
import math

import jax
import jax.numpy as jnp
from jax import lax
from jax.experimental import pallas as pl
from jax.experimental.pallas import tpu as pltpu
from jax.sharding import PartitionSpec as P

EPS = 1e-05
LOW = -1e30
TINY = 1e-30
FULL = 32766.0
F32 = jnp.float32
BF16 = jnp.bfloat16
LANES = 128
CHUNK = 8192
PIECE = 1024
VMEM = pl.BlockSpec(memory_space=pltpu.VMEM)
SMEM = pl.BlockSpec(memory_space=pltpu.SMEM)
HBM = pl.BlockSpec(memory_space=pltpu.HBM)


def call(kernel, out_shape, in_specs, scratch=(), limit=4, moved=0):
    many = isinstance(out_shape, (tuple, list))
    inner = pl.pallas_call(
        kernel,
        out_shape=out_shape,
        in_specs=in_specs,
        out_specs=[VMEM] * len(out_shape) if many else VMEM,
        scratch_shapes=list(scratch),
        compiler_params=pltpu.CompilerParams(vmem_limit_bytes=limit << 20),
        cost_estimate=pl.CostEstimate(flops=0, bytes_accessed=moved, transcendentals=0) if moved else None,
    )

    def run(*args):
        return inner(
            *(pltpu.with_memory_space_constraint(x, pltpu.HBM) if s is HBM else x for x, s in zip(args, in_specs))
        )

    return run


def dot(a, b):
    return jnp.dot(a, b, preferred_element_type=F32)


def dot_t(a, b):
    return lax.dot_general(a, b, (((1,), (1,)), ((), ())), preferred_element_type=F32)


def dot_tt(a, b):
    return lax.dot_general(a, b, (((0,), (0,)), ((), ())), preferred_element_type=F32)


def split2(x):
    high = x.astype(BF16)
    return high, (x - high.astype(F32)).astype(BF16)


def lane_split(square):
    high, low = split2(square)
    lane = lax.broadcasted_iota(jnp.int32, square.shape, 1)
    return jnp.where(lane < LANES // 2, high.astype(F32), low.astype(F32)).astype(BF16)


def lane_join(pair):
    return pair + pltpu.roll(pair, LANES // 2, 1)


def core_index():
    return lax.rem(lax.axis_index("seq"), 2)


def chip_index():
    return lax.div(lax.axis_index("seq"), 2)


def project_kernel(
    resid,
    gain,
    w_query,
    w_key,
    w_value,
    angle,
    keep,
    send,
    cos,
    sin,
    x_buf,
    gain_buf,
    q_buf,
    kv_buf,
    angle_buf,
    sems,
):
    mine = core_index()
    pairs = [
        (angle, angle_buf),
        (resid, x_buf),
        (gain, gain_buf),
        (w_key, kv_buf.at[0]),
        (w_value, kv_buf.at[1]),
    ]
    pairs += [(w_query.at[pl.ds(i * 128, 128), :], q_buf.at[pl.ds(i * 128, 128), :]) for i in range(4)]
    loads = [pltpu.make_async_copy(src, dst, sems.at[i]) for i, (src, dst) in enumerate(pairs)]
    for load in loads:
        load.start()
    loads[0].wait()
    cosine, sine = jnp.cos(angle_buf[...]), jnp.sin(angle_buf[...])
    cos[...] = jnp.concatenate([cosine, cosine], axis=1)
    sin[...] = jnp.concatenate([-sine, sine], axis=1)
    loads[1].wait()
    loads[2].wait()
    x32 = x_buf[...].astype(F32)
    x = (x32 * gain_buf[...].astype(F32)[None, :]).astype(BF16)
    square = jnp.broadcast_to(jnp.sum(x32 * x32, axis=1, keepdims=True), (32, LANES))
    for load in loads[3:]:
        load.wait()
    for target, half in ((keep, mine), (send, 1 - mine)):
        cols = pl.ds(pl.multiple_of(half * 512, LANES), 512)
        target[:, 0:512] = dot(x, q_buf[:, cols])
        target[:, 512:640] = dot(x, kv_buf[half])
        target[:, 640:768] = square


def project_pair_kernel(own, other, w1, w2, w3, copies):
    total = own[...] + other[...]
    row_log = jnp.log2(total[:, 640:768] + TINY)
    meta = [jnp.floor(row_log * 256 + 0.5)]
    meta.append(jnp.floor((row_log * 256 - meta[0]) * 16384 + 0.5))
    coded = []
    for cols in (slice(0, 512), slice(512, 640)):
        x = total[:, cols]
        grade = jnp.ceil(jnp.log2(jnp.max(jnp.abs(x), axis=1, keepdims=True) + TINY))
        coded.append(jnp.floor(x * (FULL * jnp.exp2(-grade)) + 0.5))
        meta.append(jnp.broadcast_to(grade, (32, LANES)))
    lane = lax.broadcasted_iota(jnp.int32, (32, LANES), 1)
    last = jnp.where(lane < 2, jnp.where(lane == 0, meta[0], meta[1]), jnp.where(lane == 2, meta[2], meta[3]))
    last = jnp.transpose(jnp.concatenate([last, jnp.zeros((96, LANES), F32)], axis=0))[0:8]
    heads = jnp.concatenate([coded[0][:, g * 128 : (g + 1) * 128] for g in range(4)], axis=0)
    heads = heads.astype(jnp.int32).astype(jnp.int16)
    for j in range(8):
        four = coded[1][j // 2 * 8 : j // 2 * 8 + 8]
        four = pltpu.roll(four, 4, 0) if j % 2 else four
        copies[j, 0:128, :] = heads
        copies[j, 128:144, :] = jnp.concatenate([four, last], axis=0).astype(jnp.int32).astype(jnp.int16)


def rotate_kernel(parts, cos, sin, out, steps):
    tails = [parts[j, 128:144, :].astype(jnp.int32).astype(F32) for j in range(8)]
    square = jnp.zeros((1, LANES), F32)
    for tail in tails:
        square += jnp.exp2(tail[8:9] / 256 + tail[9:10] / (256 * 16384))
    inv = lax.rsqrt(square / 8192 + EPS)
    rows = [jnp.exp2(tail[10:11]) * (inv / FULL) for tail in tails]
    rows += [jnp.exp2(tail[11:12]) * (inv / FULL) for tail in tails]
    turned = jnp.transpose(jnp.concatenate(rows + [jnp.zeros((112, LANES), F32)], axis=0))
    steps[...] = turned[0:32]

    for g in range(4):
        x = jnp.zeros((32, LANES), F32)
        for j in range(8):
            head = parts[j, g * 32 : (g + 1) * 32, :].astype(jnp.int32).astype(F32)
            x += head * steps[:, j : j + 1]
        out[g * 32 : (g + 1) * 32, :] = (x * cos[...] + pltpu.roll(x, LANES // 2, 1) * sin[...]).astype(BF16)

    chip = chip_index()
    base = pl.ds(pl.multiple_of(lax.div(chip, 2) * 8, 8), 8)

    def four(ref):
        x = ref[base, :]
        return jnp.where(lax.rem(chip, 2) == 0, x, pltpu.roll(x, 4, 0))

    step = four(steps)
    x = jnp.zeros((8, LANES), F32)
    for j in range(8):
        x += tails[j][0:8] * step[:, 8 + j : 9 + j]
    key = x * four(cos) + pltpu.roll(x, LANES // 2, 1) * four(sin)
    x = jnp.where(core_index() == 0, key, x)
    out[128:144, :] = jnp.concatenate([x, jnp.zeros((8, LANES), F32)], axis=0).astype(BF16)


def attend_kernel(
    own, other, positions, valid, keys, values, keep, send, query, shift, total_l, total_o, new_o, new_lse
):
    scale = 128.0**-0.5
    power = scale * 1.4426950408889634
    mine = core_index()
    length = valid[0]

    query[pl.ds(pl.multiple_of(mine * 128, 128), 128), :] = own[0:128, :]
    query[pl.ds(pl.multiple_of((1 - mine) * 128, 128), 128), :] = other[0:128, :]
    q = query[...]
    a, b = own[128:144, :].astype(F32), other[128:144, :].astype(F32)
    k_new = jnp.where(mine == 0, a, b).astype(BF16)
    v_new = jnp.where(mine == 0, b, a).astype(BF16)

    lane = lax.broadcasted_iota(jnp.int32, (8, 256), 1) & 31
    row = lax.broadcasted_iota(jnp.int32, (16, 256), 0)
    of_query = jnp.zeros((8, 256), jnp.int32)
    of_key = jnp.full((16, 256), 1 << 20, jnp.int32)
    for i in range(32):
        of_query = jnp.where(lane == i, positions[i], of_query)
    for i in range(4):
        of_key = jnp.where(row == i, positions[chip_index() * 4 + i], of_key)
    allowed = (of_key <= of_query[0:1, :]) & (mine == 0)
    s_new = jnp.where(allowed, dot_t(k_new, q) * scale, LOW)
    top_new = jnp.max(s_new, axis=0, keepdims=True)
    e_new = jnp.exp(s_new - top_new).astype(BF16)
    l_new = jnp.sum(e_new.astype(F32), axis=0, keepdims=True)
    lse_new = top_new + jnp.log(l_new)
    new_o[...] = dot_tt(v_new, e_new) / l_new
    new_lse[...] = jnp.broadcast_to(lse_new, (8, 256))

    def score(start, count=PIECE):
        return dot_t(keys[0, pl.ds(start, count), :], q)

    def only_valid(s, start):
        slot = lax.broadcasted_iota(jnp.int32, s.shape, 0) + start
        return jnp.where(slot < length, s, LOW)

    def weigh(s, start, carry):
        sums, o = carry
        e = jnp.exp2(s * power - shift[0:1, :]).astype(BF16)
        sums = sums + jnp.sum(e.astype(F32).reshape(PIECE // 8, 8, 256), axis=0)
        return sums, o + dot_tt(values[0, pl.ds(start, PIECE), :], e)

    def run(first, pieces, masked):
        carry = (total_l[...], total_o[...])
        starts = [pl.multiple_of(first + i * PIECE, PIECE) for i in range(pieces)]
        s = score(starts[0])
        for i in range(pieces):
            ahead = score(starts[i + 1]) if i + 1 < pieces else None
            carry = weigh(only_valid(s, starts[i]) if masked else s, starts[i], carry)
            s = ahead
        total_l[...], total_o[...] = carry

    def restart(top):
        shift[...] = jnp.broadcast_to(top * power, (8, 256))
        total_l[...] = jnp.zeros((8, 256), F32)
        total_o[...] = jnp.zeros((LANES, 256), F32)

    restart(jnp.max(only_valid(score(0, 256), 0), axis=0, keepdims=True))

    @pl.when(length == 16384)
    def _():
        run(0, 16384 // PIECE, False)

    @pl.when(length < 16384)
    def _():
        half_full = length >= CHUNK

        @pl.when(half_full)
        def _():
            run(0, CHUNK // PIECE, False)

        @pl.when(length != CHUNK)
        def _():
            run(pl.multiple_of(jnp.where(half_full, CHUNK, 0), CHUNK), CHUNK // PIECE, True)

    @pl.when(jnp.logical_not(jnp.max(total_l[...]) < 1e30))
    def _():
        pieces = lax.div(length + (PIECE - 1), PIECE)
        shift[...] = jnp.full((8, 256), LOW, F32)

        @pl.loop(0, pieces)
        def _(c):
            start = pl.multiple_of(c * PIECE, PIECE)
            top = jnp.max(only_valid(score(start), start), axis=0, keepdims=True)
            shift[...] = jnp.maximum(shift[...], top)

        restart(shift[0:1, :])

        @pl.loop(0, pieces)
        def _(c):
            run(pl.multiple_of(c * PIECE, PIECE), 1, True)

    l_old = jnp.sum(total_l[...], axis=0, keepdims=True)
    lse_old = shift[0:1, :] * math.log(2.0) + jnp.log(l_old)

    lse_new = new_lse[0:1, :]
    high = jnp.maximum(lse_old, lse_new)
    f_old = jnp.exp(lse_old - high)
    f_new = jnp.exp(lse_new - high)
    both = f_old + f_new
    o = total_o[...] * (f_old / (l_old * both)) + new_o[...] * (f_new / both)
    lse = jnp.broadcast_to(high + jnp.log(both), (8, 256))
    for target, first in ((keep, mine == 0), (send, mine != 0)):
        target[0:128, :] = jnp.where(first, o[:, 0:128], o[:, 128:256])
        target[128:136, :] = jnp.where(first, lse[:, 0:128], lse[:, 128:256])


def merge_pair_kernel(own, other, copies):
    la, lb = own[128:136, :], other[128:136, :]
    high = jnp.maximum(la, lb)
    fa, fb = jnp.exp(la - high), jnp.exp(lb - high)
    both = fa + fb
    o = (own[0:128, :] * (fa / both)[0:1] + other[0:128, :] * (fb / both)[0:1]).astype(BF16)
    lse = high + jnp.log(both)
    p0 = lse.astype(BF16).astype(F32)
    rest = lse - p0
    p1 = rest.astype(BF16).astype(F32)
    p2 = rest - p1
    row = lax.broadcasted_iota(jnp.int32, (8, LANES), 0)
    tail = jnp.where(row == 0, p0, jnp.where(row == 1, p1, p2))
    tail = jnp.concatenate([tail, jnp.zeros((8, LANES), F32)], axis=0).astype(BF16)
    for j in range(8):
        copies[j, 0:128, :] = o
        copies[j, 128:144, :] = tail


def merge_kernel(parts, attn):
    rows = []
    for j in range(8):
        tail = parts[j, 128:144, :].astype(F32)
        rows.append(tail[0:1] + tail[1:2] + tail[2:3])
    high = functools.reduce(jnp.maximum, rows)
    weights = [jnp.exp(r - high) for r in rows]
    both = functools.reduce(jnp.add, weights)
    total = parts[0, 0:128, :].astype(F32) * (weights[0] / both)
    for j in range(1, 8):
        total += parts[j, 0:128, :].astype(F32) * (weights[j] / both)
    total = jnp.transpose(total)
    for g in range(4):
        attn[:, g * 128 : (g + 1) * 128] = total[g * 32 : (g + 1) * 32].astype(BF16)


def out_kernel(own, other, w_out, copies):
    mine = core_index()
    total = jnp.zeros((32, 512), F32)
    for source, half in ((own, mine), (other, 1 - mine)):
        total += dot(source[...], w_out[pl.ds(pl.multiple_of(half * 512, LANES), 512), :])
    part = total.astype(BF16)
    for j in range(8):
        copies[j] = part


def sum_parts(parts):
    total = parts[0].astype(F32)
    for j in range(1, 8):
        total = total + parts[j].astype(F32)
    return total


def gate_up(x, w_gate, w_up, half, target):
    for i in range(2):
        cols = pl.ds(pl.multiple_of(half * 1792 + i * 896, LANES), 896)
        target[:, i * 896 : (i + 1) * 896] = dot(x, w_gate[:, cols]).astype(target.dtype)
        target[:, 1792 + i * 896 : 1792 + (i + 1) * 896] = dot(x, w_up[:, cols]).astype(target.dtype)


def gate_up_send_kernel(parts, resid, gain, w_gate, w_up, attn_out, mid, normed, square, send):
    branch = sum_parts(parts).astype(BF16)
    attn_out[...] = branch
    hidden = (resid[...].astype(F32) + branch.astype(F32)).astype(BF16)
    mid[...] = hidden
    x32 = hidden.astype(F32)
    x = (x32 * gain[...].astype(F32)[None, :]).astype(BF16)
    normed[...] = x
    total = jnp.broadcast_to(jnp.sum(x32 * x32, axis=1, keepdims=True), (32, LANES))
    square[...] = total
    gate_up(x, w_gate, w_up, 1 - core_index(), send)
    send[:, 3584:3712] = lane_split(total)


def gate_up_keep_kernel(normed, w_gate, w_up, keep):
    gate_up(normed[...], w_gate, w_up, core_index(), keep)


def gate_up_pair_kernel(keep, own_square, got, pieces):
    square = own_square[...] + lane_join(got[:, 3584:3712].astype(F32))
    high = square.astype(BF16).astype(F32)
    low = square - high
    for j in range(8):
        rows = slice((j // 2) * 8, (j // 2) * 8 + 8)
        block = []
        for base in (0, 1792):
            cols = slice(base + (j % 2) * 896, base + (j % 2 + 1) * 896)
            block.append(keep[rows, cols] + got[:, cols].astype(F32)[rows])
        pieces[j, :, 0:896] = jnp.concatenate(block, axis=0).astype(BF16)
        pieces[j, :, 896:1024] = jnp.concatenate([high[rows], low[rows]], axis=0).astype(BF16)


def act_kernel(parts, copies):
    total = sum_parts(parts)
    square = (total[0:8] + total[8:16])[:, 896:897]
    inv = lax.rsqrt(square / 8192 + EPS)
    gate = total[0:8, 0:896] * inv
    up = total[8:16, 0:896] * inv
    act = gate / (1.0 + jnp.exp(-gate)) * up
    packed = jnp.concatenate(
        [act[:, 0:512], jnp.concatenate([act[:, 512:896], jnp.zeros((8, LANES), F32)], axis=1)], axis=0
    ).astype(BF16)
    for j in range(8):
        copies[j] = packed


def down(acts, w_down, half):
    total = jnp.zeros((32, 512), F32)
    for ch in range(2):
        wide = []
        for rg in range(4):
            piece = acts[rg * 2 + ch].astype(F32)
            wide.append(jnp.concatenate([piece[0:8], piece[8:16, 0:384]], axis=1))
        act = jnp.concatenate(wide, axis=0).astype(BF16)
        rows = pl.ds(pl.multiple_of(half * 1792 + ch * 896, LANES), 896)
        total += dot(act, w_down[rows, :])
    return total


def down_own_kernel(acts, w_down, part):
    part[...] = down(acts, w_down, core_index())


def down_other_kernel(own, acts, w_down, copies):
    part = (own[...] + down(acts, w_down, 1 - core_index())).astype(BF16)
    for j in range(8):
        copies[j] = part


def final_kernel(parts, mid, layer_out):
    layer_out[...] = (mid[...].astype(F32) + sum_parts(parts)).astype(BF16)


def body(
    resid,
    attn_gain,
    ffn_gain,
    w_query,
    w_key,
    w_value,
    w_out,
    rope_angle,
    positions,
    cache_keys,
    cache_values,
    valid_lengths,
    w_gate,
    w_up,
    w_down,
):
    shape = jax.ShapeDtypeStruct
    near = pltpu.VMEM
    same_core = [[2 * j + c for j in range(8)] for c in range(2)]
    swap = [(i, i ^ 1) for i in range(16)]

    def to_other_core(x):
        return lax.ppermute(x, "seq", swap)

    def over_chips(x):
        return lax.all_to_all(x, "seq", 0, 0, axis_index_groups=same_core)

    def over_tp(x):
        return lax.all_to_all(x, "tp", 0, 0)

    table = near((32, LANES), F32)
    keep, send, cos, sin = call(
        project_kernel,
        (near((32, 768), F32), near((32, 768), F32), table, table),
        [HBM] * 6,
        scratch=[
            pltpu.VMEM((32, 512), BF16),
            pltpu.VMEM((512,), BF16),
            pltpu.VMEM((512, 1024), BF16),
            pltpu.VMEM((2, 512, LANES), BF16),
            pltpu.VMEM((32, 64), F32),
            pltpu.SemaphoreType.DMA((9,)),
        ],
    )(resid, attn_gain, w_query, w_key, w_value, rope_angle)
    copies = call(project_pair_kernel, near((8, 144, LANES), jnp.int16), [VMEM] * 2 + [HBM] * 3)(
        keep, to_other_core(send), w_gate, w_up, w_down
    )
    turned = call(rotate_kernel, near((144, LANES), BF16), [VMEM] * 3, scratch=[pltpu.VMEM((32, LANES), F32)])(
        over_chips(copies), cos, sin
    )

    keep, send = call(
        attend_kernel,
        (near((136, LANES), F32), near((136, LANES), F32)),
        [VMEM] * 2 + [SMEM] * 2 + [VMEM] * 2,
        scratch=[
            pltpu.VMEM((256, LANES), BF16),
            pltpu.VMEM((8, 256), F32),
            pltpu.VMEM((8, 256), F32),
            pltpu.VMEM((LANES, 256), F32),
            pltpu.VMEM((LANES, 256), F32),
            pltpu.VMEM((8, 256), F32),
        ],
        limit=24,
    )(turned, to_other_core(turned), positions, valid_lengths, cache_keys, cache_values)
    copies = call(merge_pair_kernel, near((8, 144, LANES), BF16), [VMEM] * 2)(keep, to_other_core(send))
    attn = call(merge_kernel, near((32, 512), BF16), [VMEM])(over_chips(copies))
    copies = call(out_kernel, near((8, 32, 512), BF16), [VMEM] * 3)(attn, to_other_core(attn), w_out)
    parts = over_tp(copies)

    attn_out, mid, normed, square, send = call(
        gate_up_send_kernel,
        (shape((32, 512), BF16), near((32, 512), BF16), near((32, 512), BF16), table, near((32, 3712), BF16)),
        [VMEM] * 5,
        limit=12,
    )(parts, resid, ffn_gain, w_gate, w_up)
    got = to_other_core(send)
    keep = call(gate_up_keep_kernel, near((32, 3584), F32), [VMEM] * 3, limit=12)(normed, w_gate, w_up)
    pieces = call(gate_up_pair_kernel, near((8, 16, 1024), BF16), [VMEM] * 3)(keep, square, got)
    parts = over_chips(pieces)
    copies = call(act_kernel, near((8, 16, 512), BF16), [VMEM])(parts)
    acts = over_chips(copies)
    got = to_other_core(acts)
    part = call(down_own_kernel, near((32, 512), F32), [VMEM] * 2, limit=8)(acts, w_down)
    copies = call(down_other_kernel, near((8, 32, 512), BF16), [VMEM] * 3, limit=8)(part, got, w_down)
    parts = over_tp(copies)
    layer_out = call(final_kernel, shape((32, 512), BF16), [VMEM] * 2)(parts, mid)
    return (attn_out, layer_out)


def solution(mesh):
    in_specs = (
        P(None, "seq"),
        P("seq"),
        P("seq"),
        P("seq", "tp"),
        P("seq", "tp"),
        P("seq", "tp"),
        P("tp", "seq"),
        P(),
        P(),
        P("tp", "seq", None),
        P("tp", "seq", None),
        P("seq"),
        P("seq", "tp"),
        P("seq", "tp"),
        P("tp", "seq"),
    )
    out_specs = (P(None, "seq"), P(None, "seq"))
    return jax.shard_map(body, mesh=mesh, in_specs=in_specs, out_specs=out_specs, check_vma=False)
```

```python
import functools
import math

import jax
import jax.numpy as jnp
from jax import lax
from jax.experimental import pallas as pl
from jax.experimental.pallas import tpu as pltpu
from jax.sharding import PartitionSpec as P

EPS = 1e-05
LOW = -1e30
TINY = 1e-30
FULL = 32766.0
F32 = jnp.float32
BF16 = jnp.bfloat16
LANES = 128
CHUNK = 8192
PIECE = 1024
VMEM = pl.BlockSpec(memory_space=pltpu.VMEM)
SMEM = pl.BlockSpec(memory_space=pltpu.SMEM)
HBM = pl.BlockSpec(memory_space=pltpu.HBM)


def call(kernel, out_shape, in_specs, scratch=(), limit=4, out_specs=None):
    many = isinstance(out_shape, (tuple, list))
    inner = pl.pallas_call(
        kernel,
        out_shape=out_shape,
        in_specs=in_specs,
        out_specs=out_specs or ([VMEM] * len(out_shape) if many else VMEM),
        scratch_shapes=list(scratch),
        compiler_params=pltpu.CompilerParams(vmem_limit_bytes=limit << 20),
    )

    def run(*args):
        return inner(
            *(pltpu.with_memory_space_constraint(x, pltpu.HBM) if s is HBM else x for x, s in zip(args, in_specs))
        )

    return run


def dot(a, b):
    return jnp.dot(a, b, preferred_element_type=F32)


def dot_t(a, b):
    return lax.dot_general(a, b, (((1,), (1,)), ((), ())), preferred_element_type=F32)


def dot_tt(a, b):
    return lax.dot_general(a, b, (((0,), (0,)), ((), ())), preferred_element_type=F32)


def split2(x):
    high = x.astype(BF16)
    return high, (x - high.astype(F32)).astype(BF16)


def lane_split(square):
    high, low = split2(square)
    lane = lax.broadcasted_iota(jnp.int32, square.shape, 1)
    return jnp.where(lane < LANES // 2, high.astype(F32), low.astype(F32)).astype(BF16)


def lane_join(pair):
    return pair + pltpu.roll(pair, LANES // 2, 1)


def core_index():
    return lax.rem(lax.axis_index("seq"), 2)


def chip_index():
    return lax.div(lax.axis_index("seq"), 2)


def project_kernel(
    resid,
    gain,
    w_query,
    w_key,
    w_value,
    angle,
    keep,
    send,
    cos,
    sin,
    x_buf,
    gain_buf,
    q_buf,
    kv_buf,
    angle_buf,
    sems,
):
    mine = core_index()
    pairs = [
        (angle, angle_buf),
        (resid, x_buf),
        (gain, gain_buf),
        (w_key, kv_buf.at[0]),
        (w_value, kv_buf.at[1]),
    ]
    pairs += [(w_query.at[pl.ds(i * 128, 128), :], q_buf.at[pl.ds(i * 128, 128), :]) for i in range(4)]
    loads = [pltpu.make_async_copy(src, dst, sems.at[i]) for i, (src, dst) in enumerate(pairs)]
    for load in loads:
        load.start()
    loads[0].wait()
    cosine, sine = jnp.cos(angle_buf[...]), jnp.sin(angle_buf[...])
    cos[...] = jnp.concatenate([cosine, cosine], axis=1)
    sin[...] = jnp.concatenate([-sine, sine], axis=1)
    loads[1].wait()
    loads[2].wait()
    x32 = x_buf[...].astype(F32)
    x = (x32 * gain_buf[...].astype(F32)[None, :]).astype(BF16)
    square = jnp.broadcast_to(jnp.sum(x32 * x32, axis=1, keepdims=True), (32, LANES))
    loads[3].wait()
    loads[4].wait()
    for target, half in ((keep, mine), (send, 1 - mine)):
        target[:, 512:640] = dot(x, kv_buf[half])
        target[:, 640:768] = square
    total = jnp.zeros((32, 1024), F32)
    for i in range(4):
        loads[5 + i].wait()
        total += dot(x[:, i * 128 : (i + 1) * 128], q_buf[i * 128 : (i + 1) * 128, :])
    first, second = total[:, 0:512], total[:, 512:1024]
    keep[:, 0:512] = jnp.where(mine == 0, first, second)
    send[:, 0:512] = jnp.where(mine == 0, second, first)


def project_pair_kernel(own, other, w1, w2, w3, copies):
    total = own[...] + other[...]
    row_log = jnp.log2(total[:, 640:768] + TINY)
    meta = [jnp.floor(row_log * 256 + 0.5)]
    meta.append(jnp.floor((row_log * 256 - meta[0]) * 16384 + 0.5))
    coded = []
    for cols in (slice(0, 512), slice(512, 640)):
        x = total[:, cols]
        grade = jnp.ceil(jnp.log2(jnp.max(jnp.abs(x), axis=1, keepdims=True) + TINY))
        coded.append(jnp.floor(x * (FULL * jnp.exp2(-grade)) + 0.5))
        meta.append(jnp.broadcast_to(grade, (32, LANES)))
    lane = lax.broadcasted_iota(jnp.int32, (32, LANES), 1)
    last = jnp.where(lane < 2, jnp.where(lane == 0, meta[0], meta[1]), jnp.where(lane == 2, meta[2], meta[3]))
    last = jnp.transpose(jnp.concatenate([last, jnp.zeros((96, LANES), F32)], axis=0))[0:8]
    heads = jnp.concatenate([coded[0][:, g * 128 : (g + 1) * 128] for g in range(4)], axis=0)
    heads = heads.astype(jnp.int32).astype(jnp.int16)
    for j in range(8):
        four = coded[1][j // 2 * 8 : j // 2 * 8 + 8]
        four = pltpu.roll(four, 4, 0) if j % 2 else four
        copies[j, 0:128, :] = heads
        copies[j, 128:144, :] = jnp.concatenate([four, last], axis=0).astype(jnp.int32).astype(jnp.int16)


def rotate_kernel(parts, cos, sin, out, steps):
    tails = [parts[j, 128:144, :].astype(jnp.int32).astype(F32) for j in range(8)]
    square = jnp.zeros((1, LANES), F32)
    for tail in tails:
        square += jnp.exp2(tail[8:9] / 256 + tail[9:10] / (256 * 16384))
    inv = lax.rsqrt(square / 8192 + EPS)
    rows = [jnp.exp2(tail[10:11]) * (inv / FULL) for tail in tails]
    rows += [jnp.exp2(tail[11:12]) * (inv / FULL) for tail in tails]
    turned = jnp.transpose(jnp.concatenate(rows + [jnp.zeros((112, LANES), F32)], axis=0))
    steps[...] = turned[0:32]
    wide = [jnp.broadcast_to(turned[0:32, j : j + 1], (32, LANES)) for j in range(8)]

    for g in range(4):
        x = jnp.zeros((32, LANES), F32)
        for j in range(8):
            head = parts[j, g * 32 : (g + 1) * 32, :].astype(jnp.int32).astype(F32)
            x += head * wide[j]
        out[g * 32 : (g + 1) * 32, :] = (x * cos[...] + pltpu.roll(x, LANES // 2, 1) * sin[...]).astype(BF16)

    chip = chip_index()
    base = pl.ds(pl.multiple_of(lax.div(chip, 2) * 8, 8), 8)

    def four(ref):
        x = ref[base, :]
        return jnp.where(lax.rem(chip, 2) == 0, x, pltpu.roll(x, 4, 0))

    step = four(steps)
    x = jnp.zeros((8, LANES), F32)
    for j in range(8):
        x += tails[j][0:8] * step[:, 8 + j : 9 + j]
    key = x * four(cos) + pltpu.roll(x, LANES // 2, 1) * four(sin)
    x = jnp.where(core_index() == 0, key, x)
    out[128:144, :] = jnp.concatenate([x, jnp.zeros((8, LANES), F32)], axis=0).astype(BF16)


def attend_kernel(
    own, other, positions, valid, keys, values, keep, send, query, shift, total_l, total_o, new_o, new_lse
):
    scale = 128.0**-0.5
    power = scale * 1.4426950408889634
    mine = core_index()
    length = valid[0]

    query[pl.ds(pl.multiple_of(mine * 128, 128), 128), :] = own[0:128, :]
    query[pl.ds(pl.multiple_of((1 - mine) * 128, 128), 128), :] = other[0:128, :]
    q = query[...]
    a, b = own[128:144, :].astype(F32), other[128:144, :].astype(F32)
    k_new = jnp.where(mine == 0, a, b).astype(BF16)
    v_new = jnp.where(mine == 0, b, a).astype(BF16)

    lane = lax.broadcasted_iota(jnp.int32, (8, 256), 1) & 31
    row = lax.broadcasted_iota(jnp.int32, (16, 256), 0)
    of_query = jnp.zeros((8, 256), jnp.int32)
    of_key = jnp.full((16, 256), 1 << 20, jnp.int32)
    for i in range(32):
        of_query = jnp.where(lane == i, positions[i], of_query)
    for i in range(4):
        of_key = jnp.where(row == i, positions[chip_index() * 4 + i], of_key)
    allowed = (of_key <= of_query[0:1, :]) & (mine == 0)
    s_new = jnp.where(allowed, dot_t(k_new, q) * scale, LOW)
    top_new = jnp.max(s_new, axis=0, keepdims=True)
    e_new = jnp.exp(s_new - top_new).astype(BF16)
    l_new = jnp.sum(e_new.astype(F32), axis=0, keepdims=True)
    lse_new = top_new + jnp.log(l_new)
    new_o[...] = dot_tt(v_new, e_new) / l_new
    new_lse[...] = jnp.broadcast_to(lse_new, (8, 256))

    def score(start, count=PIECE):
        return dot_t(keys[0, pl.ds(start, count), :], q)

    def only_valid(s, start):
        slot = lax.broadcasted_iota(jnp.int32, s.shape, 0) + start
        return jnp.where(slot < length, s, LOW)

    def weigh(s, start, carry):
        sums, o = carry
        e = jnp.exp2(s * power - shift[0:1, :]).astype(BF16)
        sums = sums + jnp.sum(e.astype(F32).reshape(PIECE // 8, 8, 256), axis=0)
        return sums, o + dot_tt(values[0, pl.ds(start, PIECE), :], e)

    def run(first, pieces, masked):
        carry = (total_l[...], total_o[...])
        starts = [pl.multiple_of(first + i * PIECE, PIECE) for i in range(pieces)]
        s = score(starts[0])
        for i in range(pieces):
            ahead = score(starts[i + 1]) if i + 1 < pieces else None
            carry = weigh(only_valid(s, starts[i]) if masked else s, starts[i], carry)
            s = ahead
        total_l[...], total_o[...] = carry

    def restart(top):
        shift[...] = jnp.broadcast_to(top * power, (8, 256))
        total_l[...] = jnp.zeros((8, 256), F32)
        total_o[...] = jnp.zeros((LANES, 256), F32)

    restart(jnp.max(only_valid(score(0, 256), 0), axis=0, keepdims=True))

    @pl.when(length == 16384)
    def _():
        run(0, 16384 // PIECE, False)

    @pl.when(length < 16384)
    def _():
        half_full = length >= CHUNK

        @pl.when(half_full)
        def _():
            run(0, CHUNK // PIECE, False)

        @pl.when(length != CHUNK)
        def _():
            run(pl.multiple_of(jnp.where(half_full, CHUNK, 0), CHUNK), CHUNK // PIECE, True)

    def finish():
        l_old = jnp.sum(total_l[...], axis=0, keepdims=True)
        lse_old = shift[0:1, :] * math.log(2.0) + jnp.log(l_old)
        lse_new = new_lse[0:1, :]
        high = jnp.maximum(lse_old, lse_new)
        f_old = jnp.exp(lse_old - high)
        f_new = jnp.exp(lse_new - high)
        both = f_old + f_new
        o = total_o[...] * (f_old / (l_old * both)) + new_o[...] * (f_new / both)
        lse = jnp.broadcast_to(high + jnp.log(both), (8, 256))
        for target, first in ((keep, mine == 0), (send, mine != 0)):
            target[0:128, :] = jnp.where(first, o[:, 0:128], o[:, 128:256])
            target[128:136, :] = jnp.where(first, lse[:, 0:128], lse[:, 128:256])

    finish()

    @pl.when(jnp.logical_not(jnp.max(total_l[...]) < 1e30))
    def _():
        pieces = lax.div(length + (PIECE - 1), PIECE)
        shift[...] = jnp.full((8, 256), LOW, F32)

        @pl.loop(0, pieces)
        def _(c):
            start = pl.multiple_of(c * PIECE, PIECE)
            top = jnp.max(only_valid(score(start), start), axis=0, keepdims=True)
            shift[...] = jnp.maximum(shift[...], top)

        restart(shift[0:1, :])

        @pl.loop(0, pieces)
        def _(c):
            run(pl.multiple_of(c * PIECE, PIECE), 1, True)

        finish()


def merge_pair_kernel(own, other, copies):
    la, lb = own[128:136, :], other[128:136, :]
    high = jnp.maximum(la, lb)
    fa, fb = jnp.exp(la - high), jnp.exp(lb - high)
    both = fa + fb
    o = (own[0:128, :] * (fa / both)[0:1] + other[0:128, :] * (fb / both)[0:1]).astype(BF16)
    lse = high + jnp.log(both)
    p0 = lse.astype(BF16).astype(F32)
    rest = lse - p0
    p1 = rest.astype(BF16).astype(F32)
    p2 = rest - p1
    row = lax.broadcasted_iota(jnp.int32, (8, LANES), 0)
    tail = jnp.where(row == 0, p0, jnp.where(row == 1, p1, p2))
    tail = jnp.concatenate([tail, jnp.zeros((8, LANES), F32)], axis=0).astype(BF16)
    for j in range(8):
        copies[j, 0:128, :] = o
        copies[j, 128:144, :] = tail


def merge_kernel(parts, attn):
    rows = []
    for j in range(8):
        tail = parts[j, 128:144, :].astype(F32)
        rows.append(tail[0:1] + tail[1:2] + tail[2:3])
    high = functools.reduce(jnp.maximum, rows)
    weights = [jnp.exp(r - high) for r in rows]
    both = functools.reduce(jnp.add, weights)
    total = parts[0, 0:128, :].astype(F32) * (weights[0] / both)
    for j in range(1, 8):
        total += parts[j, 0:128, :].astype(F32) * (weights[j] / both)
    total = jnp.transpose(total)
    for g in range(4):
        attn[:, g * 128 : (g + 1) * 128] = total[g * 32 : (g + 1) * 32].astype(BF16)


def out_kernel(own, other, w_out, copies):
    mine = core_index()
    total = jnp.zeros((32, 512), F32)
    for source, half in ((own, mine), (other, 1 - mine)):
        total += dot(source[...], w_out[pl.ds(pl.multiple_of(half * 512, LANES), 512), :])
    part = total.astype(BF16)
    for j in range(8):
        copies[j] = part


def sum_parts(parts):
    total = parts[0].astype(F32)
    for j in range(1, 8):
        total = total + parts[j].astype(F32)
    return total


def gate_up(x, w_gate, w_up, half, target):
    for i in range(2):
        cols = pl.ds(pl.multiple_of(half * 1792 + i * 896, LANES), 896)
        target[:, i * 896 : (i + 1) * 896] = dot(x, w_gate[:, cols]).astype(target.dtype)
        target[:, 1792 + i * 896 : 1792 + (i + 1) * 896] = dot(x, w_up[:, cols]).astype(target.dtype)


def gate_up_send_kernel(parts, resid, gain, w_gate, w_up, branch_out, mid, normed, square, send):
    branch = sum_parts(parts).astype(BF16)
    branch_out[...] = branch
    hidden = (resid[...].astype(F32) + branch.astype(F32)).astype(BF16)
    mid[...] = hidden
    x32 = hidden.astype(F32)
    x = (x32 * gain[...].astype(F32)[None, :]).astype(BF16)
    normed[...] = x
    total = jnp.broadcast_to(jnp.sum(x32 * x32, axis=1, keepdims=True), (32, LANES))
    square[...] = total
    gate_up(x, w_gate, w_up, 1 - core_index(), send)
    send[:, 3584:3712] = lane_split(total)


def gate_up_keep_kernel(normed, branch, w_gate, w_up, keep, attn_out, sem):
    out = pltpu.make_async_copy(branch, attn_out, sem)
    out.start()
    gate_up(normed[...], w_gate, w_up, core_index(), keep)
    out.wait()


def gate_up_pair_kernel(keep, own_square, got, pieces):
    square = own_square[...] + lane_join(got[:, 3584:3712].astype(F32))
    high = square.astype(BF16).astype(F32)
    low = square - high
    for j in range(8):
        rows = slice((j // 2) * 8, (j // 2) * 8 + 8)
        block = []
        for base in (0, 1792):
            cols = slice(base + (j % 2) * 896, base + (j % 2 + 1) * 896)
            block.append(keep[rows, cols] + got[:, cols].astype(F32)[rows])
        pieces[j, :, 0:896] = jnp.concatenate(block, axis=0).astype(BF16)
        pieces[j, :, 896:1024] = jnp.concatenate([high[rows], low[rows]], axis=0).astype(BF16)


def act_kernel(parts, copies):
    total = sum_parts(parts)
    square = (total[0:8] + total[8:16])[:, 896:897]
    inv = lax.rsqrt(square / 8192 + EPS)
    gate = total[0:8, 0:896] * inv
    up = total[8:16, 0:896] * inv
    act = gate / (1.0 + jnp.exp(-gate)) * up
    packed = jnp.concatenate(
        [act[:, 0:512], jnp.concatenate([act[:, 512:896], jnp.zeros((8, LANES), F32)], axis=1)], axis=0
    ).astype(BF16)
    for j in range(8):
        copies[j] = packed


def down(acts, w_down, half):
    total = jnp.zeros((32, 512), F32)
    for ch in range(2):
        wide = []
        for rg in range(4):
            piece = acts[rg * 2 + ch].astype(F32)
            wide.append(jnp.concatenate([piece[0:8], piece[8:16, 0:384]], axis=1))
        act = jnp.concatenate(wide, axis=0).astype(BF16)
        rows = pl.ds(pl.multiple_of(half * 1792 + ch * 896, LANES), 896)
        total += dot(act, w_down[rows, :])
    return total


def down_own_kernel(acts, w_down, part):
    part[...] = down(acts, w_down, core_index())


def down_other_kernel(own, acts, w_down, copies):
    part = (own[...] + down(acts, w_down, 1 - core_index())).astype(BF16)
    for j in range(8):
        copies[j] = part


def final_kernel(parts, mid, layer_out):
    layer_out[...] = (mid[...].astype(F32) + sum_parts(parts)).astype(BF16)


def body(
    resid,
    attn_gain,
    ffn_gain,
    w_query,
    w_key,
    w_value,
    w_out,
    rope_angle,
    positions,
    cache_keys,
    cache_values,
    valid_lengths,
    w_gate,
    w_up,
    w_down,
):
    shape = jax.ShapeDtypeStruct
    near = pltpu.VMEM
    same_core = [[2 * j + c for j in range(8)] for c in range(2)]
    swap = [(i, i ^ 1) for i in range(16)]

    def to_other_core(x):
        return lax.ppermute(x, "seq", swap)

    def over_chips(x):
        return lax.all_to_all(x, "seq", 0, 0, axis_index_groups=same_core)

    def over_tp(x):
        return lax.all_to_all(x, "tp", 0, 0)

    table = near((32, LANES), F32)
    keep, send, cos, sin = call(
        project_kernel,
        (near((32, 768), F32), near((32, 768), F32), table, table),
        [HBM] * 6,
        scratch=[
            pltpu.VMEM((32, 512), BF16),
            pltpu.VMEM((512,), BF16),
            pltpu.VMEM((512, 1024), BF16),
            pltpu.VMEM((2, 512, LANES), BF16),
            pltpu.VMEM((32, 64), F32),
            pltpu.SemaphoreType.DMA((9,)),
        ],
    )(resid, attn_gain, w_query, w_key, w_value, rope_angle)
    copies = call(project_pair_kernel, near((8, 144, LANES), jnp.int16), [VMEM] * 2 + [HBM] * 3)(
        keep, to_other_core(send), w_gate, w_up, w_down
    )
    turned = call(rotate_kernel, near((144, LANES), BF16), [VMEM] * 3, scratch=[pltpu.VMEM((32, LANES), F32)])(
        over_chips(copies), cos, sin
    )

    keep, send = call(
        attend_kernel,
        (near((136, LANES), F32), near((136, LANES), F32)),
        [VMEM] * 2 + [SMEM] * 2 + [VMEM] * 2,
        scratch=[
            pltpu.VMEM((256, LANES), BF16),
            pltpu.VMEM((8, 256), F32),
            pltpu.VMEM((8, 256), F32),
            pltpu.VMEM((LANES, 256), F32),
            pltpu.VMEM((LANES, 256), F32),
            pltpu.VMEM((8, 256), F32),
        ],
        limit=24,
    )(turned, to_other_core(turned), positions, valid_lengths, cache_keys, cache_values)
    copies = call(merge_pair_kernel, near((8, 144, LANES), BF16), [VMEM] * 2)(keep, to_other_core(send))
    attn = call(merge_kernel, near((32, 512), BF16), [VMEM])(over_chips(copies))
    copies = call(out_kernel, near((8, 32, 512), BF16), [VMEM] * 3)(attn, to_other_core(attn), w_out)
    parts = over_tp(copies)

    branch, mid, normed, square, send = call(
        gate_up_send_kernel,
        (near((32, 512), BF16), near((32, 512), BF16), near((32, 512), BF16), table, near((32, 3712), BF16)),
        [VMEM] * 5,
        limit=12,
    )(parts, resid, ffn_gain, w_gate, w_up)
    got = to_other_core(send)
    keep, attn_out = call(
        gate_up_keep_kernel,
        (near((32, 3584), F32), shape((32, 512), BF16)),
        [VMEM] * 4,
        scratch=[pltpu.SemaphoreType.DMA],
        limit=12,
        out_specs=[VMEM, HBM],
    )(normed, branch, w_gate, w_up)
    pieces = call(gate_up_pair_kernel, near((8, 16, 1024), BF16), [VMEM] * 3)(keep, square, got)
    parts = over_chips(pieces)
    copies = call(act_kernel, near((8, 16, 512), BF16), [VMEM])(parts)
    acts = over_chips(copies)
    got = to_other_core(acts)
    part = call(down_own_kernel, near((32, 512), F32), [VMEM] * 2, limit=8)(acts, w_down)
    copies = call(down_other_kernel, near((8, 32, 512), BF16), [VMEM] * 3, limit=8)(part, got, w_down)
    parts = over_tp(copies)
    layer_out = call(final_kernel, shape((32, 512), BF16), [VMEM] * 2)(parts, mid)
    return (attn_out, layer_out)


def solution(mesh):
    in_specs = (
        P(None, "seq"),
        P("seq"),
        P("seq"),
        P("seq", "tp"),
        P("seq", "tp"),
        P("seq", "tp"),
        P("tp", "seq"),
        P(),
        P(),
        P("tp", "seq", None),
        P("tp", "seq", None),
        P("seq"),
        P("seq", "tp"),
        P("seq", "tp"),
        P("tp", "seq"),
    )
    out_specs = (P(None, "seq"), P(None, "seq"))
    return jax.shard_map(body, mesh=mesh, in_specs=in_specs, out_specs=out_specs, check_vma=False)
```

```python
import functools
import math

import jax
import jax.numpy as jnp
from jax import lax
from jax.experimental import pallas as pl
from jax.experimental.pallas import tpu as pltpu
from jax.sharding import PartitionSpec as P

EPS = 1e-05
LOW = -1e30
F32 = jnp.float32
BF16 = jnp.bfloat16
LANES = 128
CHUNK = 8192
PIECE = 1024
VMEM = pl.BlockSpec(memory_space=pltpu.VMEM)
SMEM = pl.BlockSpec(memory_space=pltpu.SMEM)
HBM = pl.BlockSpec(memory_space=pltpu.HBM)


def call(kernel, out_shape, in_specs, scratch=(), limit=4, out_specs=None):
    many = isinstance(out_shape, (tuple, list))
    inner = pl.pallas_call(
        kernel,
        out_shape=out_shape,
        in_specs=in_specs,
        out_specs=out_specs or ([VMEM] * len(out_shape) if many else VMEM),
        scratch_shapes=list(scratch),
        compiler_params=pltpu.CompilerParams(vmem_limit_bytes=limit << 20),
    )

    def run(*args):
        return inner(
            *(pltpu.with_memory_space_constraint(x, pltpu.HBM) if s is HBM else x for x, s in zip(args, in_specs))
        )

    return run


def dot(a, b):
    return jnp.dot(a, b, preferred_element_type=F32)


def dot_t(a, b):
    return lax.dot_general(a, b, (((1,), (1,)), ((), ())), preferred_element_type=F32)


def dot_tt(a, b):
    return lax.dot_general(a, b, (((0,), (0,)), ((), ())), preferred_element_type=F32)


def split2(x):
    high = x.astype(BF16)
    return high, (x - high.astype(F32)).astype(BF16)


def lane_split(square):
    high, low = split2(square)
    lane = lax.broadcasted_iota(jnp.int32, square.shape, 1)
    return jnp.where(lane < LANES // 2, high.astype(F32), low.astype(F32)).astype(BF16)


def lane_join(pair):
    return pair + pltpu.roll(pair, LANES // 2, 1)


def core_index():
    return lax.rem(lax.axis_index("seq"), 2)


def chip_index():
    return lax.div(lax.axis_index("seq"), 2)


def project_kernel(
    resid,
    gain,
    w_query,
    w_key,
    w_value,
    angle,
    keep,
    send,
    cos,
    sin,
    x_buf,
    gain_buf,
    q_buf,
    kv_buf,
    angle_buf,
    sems,
):
    mine = core_index()
    pairs = [
        (angle, angle_buf),
        (resid, x_buf),
        (gain, gain_buf),
        (w_key, kv_buf.at[0]),
        (w_value, kv_buf.at[1]),
    ]
    pairs += [(w_query.at[pl.ds(i * 128, 128), :], q_buf.at[pl.ds(i * 128, 128), :]) for i in range(4)]
    loads = [pltpu.make_async_copy(src, dst, sems.at[i]) for i, (src, dst) in enumerate(pairs)]
    for load in loads:
        load.start()
    loads[0].wait()
    cosine, sine = jnp.cos(angle_buf[...]), jnp.sin(angle_buf[...])
    cos[...] = jnp.concatenate([cosine, cosine], axis=1)
    sin[...] = jnp.concatenate([-sine, sine], axis=1)
    loads[1].wait()
    loads[2].wait()
    x32 = x_buf[...].astype(F32)
    x = (x32 * gain_buf[...].astype(F32)[None, :]).astype(BF16)
    square = jnp.broadcast_to(jnp.sum(x32 * x32, axis=1, keepdims=True), (32, LANES))
    loads[3].wait()
    loads[4].wait()
    for target, half in ((keep, mine), (send, 1 - mine)):
        target[:, 512:640] = dot(x, kv_buf[half])
        target[:, 640:768] = square
    total = jnp.zeros((32, 1024), F32)
    for i in range(4):
        loads[5 + i].wait()
        total += dot(x[:, i * 128 : (i + 1) * 128], q_buf[i * 128 : (i + 1) * 128, :])
    first, second = total[:, 0:512], total[:, 512:1024]
    keep[:, 0:512] = jnp.where(mine == 0, first, second)
    send[:, 0:512] = jnp.where(mine == 0, second, first)


def project_pair_kernel(own, other, w1, w2, w3, copies):
    total = own[...] + other[...]
    square = jnp.transpose(jnp.concatenate([total[:, 640:768], jnp.zeros((96, LANES), F32)], axis=0))[0:8]
    heads = jnp.concatenate([total[:, g * 128 : (g + 1) * 128] for g in range(4)], axis=0)
    row = lax.broadcasted_iota(jnp.int32, (8, LANES), 0)
    for j in range(8):
        four = total[j // 2 * 8 : j // 2 * 8 + 8, 512:640]
        four = pltpu.roll(four, 4, 0) if j % 2 else four
        copies[j, 0:128, :] = heads
        copies[j, 128:136, :] = jnp.where(row < 4, four, square)


def rotate_kernel(parts, cos, sin, out, factor):
    total = sum_parts(parts)
    tail = total[128:136]
    inv = jnp.broadcast_to(lax.rsqrt(tail[4:5] / 8192 + EPS), (LANES, LANES))
    inv = jnp.transpose(inv)[0:32]
    factor[...] = inv

    for g in range(4):
        x = total[g * 32 : (g + 1) * 32] * inv
        out[g * 32 : (g + 1) * 32, :] = (x * cos[...] + pltpu.roll(x, LANES // 2, 1) * sin[...]).astype(BF16)

    chip = chip_index()
    base = pl.ds(pl.multiple_of(lax.div(chip, 2) * 8, 8), 8)

    def four(ref):
        x = ref[base, :]
        return jnp.where(lax.rem(chip, 2) == 0, x, pltpu.roll(x, 4, 0))

    x = tail * four(factor)
    key = x * four(cos) + pltpu.roll(x, LANES // 2, 1) * four(sin)
    x = jnp.where(core_index() == 0, key, x)
    out[128:144, :] = jnp.concatenate([x, jnp.zeros((8, LANES), F32)], axis=0).astype(BF16)


def attend_kernel(
    own, other, positions, valid, keys, values, keep, send, query, shift, total_l, total_o, new_o, new_lse
):
    scale = 128.0**-0.5
    power = scale * 1.4426950408889634
    mine = core_index()
    length = valid[0]

    query[pl.ds(pl.multiple_of(mine * 128, 128), 128), :] = own[0:128, :]
    query[pl.ds(pl.multiple_of((1 - mine) * 128, 128), 128), :] = other[0:128, :]
    q = query[...]
    a, b = own[128:144, :].astype(F32), other[128:144, :].astype(F32)
    k_new = jnp.where(mine == 0, a, b).astype(BF16)
    v_new = jnp.where(mine == 0, b, a).astype(BF16)

    lane = lax.broadcasted_iota(jnp.int32, (8, 256), 1) & 31
    row = lax.broadcasted_iota(jnp.int32, (16, 256), 0)
    of_query = jnp.zeros((8, 256), jnp.int32)
    of_key = jnp.full((16, 256), 1 << 20, jnp.int32)
    for i in range(32):
        of_query = jnp.where(lane == i, positions[i], of_query)
    for i in range(4):
        of_key = jnp.where(row == i, positions[chip_index() * 4 + i], of_key)
    allowed = (of_key <= of_query[0:1, :]) & (mine == 0)
    s_new = jnp.where(allowed, dot_t(k_new, q) * scale, LOW)
    top_new = jnp.max(s_new, axis=0, keepdims=True)
    e_new = jnp.exp(s_new - top_new).astype(BF16)
    l_new = jnp.sum(e_new.astype(F32), axis=0, keepdims=True)
    lse_new = top_new + jnp.log(l_new)
    new_o[...] = dot_tt(v_new, e_new) / l_new
    new_lse[...] = jnp.broadcast_to(lse_new, (8, 256))

    def score(start, count=PIECE):
        return dot_t(keys[0, pl.ds(start, count), :], q)

    def only_valid(s, start):
        slot = lax.broadcasted_iota(jnp.int32, s.shape, 0) + start
        return jnp.where(slot < length, s, LOW)

    def weigh(s, start, carry):
        sums, o = carry
        e = jnp.exp2(s * power - shift[0:1, :]).astype(BF16)
        sums = sums + jnp.sum(e.astype(F32).reshape(PIECE // 8, 8, 256), axis=0)
        return sums, o + dot_tt(values[0, pl.ds(start, PIECE), :], e)

    def run(first, pieces, masked):
        carry = (total_l[...], total_o[...])
        starts = [pl.multiple_of(first + i * PIECE, PIECE) for i in range(pieces)]
        s = score(starts[0])
        for i in range(pieces):
            ahead = score(starts[i + 1]) if i + 1 < pieces else None
            carry = weigh(only_valid(s, starts[i]) if masked else s, starts[i], carry)
            s = ahead
        total_l[...], total_o[...] = carry

    def restart(top):
        shift[...] = jnp.broadcast_to(top * power, (8, 256))
        total_l[...] = jnp.zeros((8, 256), F32)
        total_o[...] = jnp.zeros((LANES, 256), F32)

    restart(jnp.max(only_valid(score(0, 256), 0), axis=0, keepdims=True))

    @pl.when(length == 16384)
    def _():
        run(0, 16384 // PIECE, False)

    @pl.when(length < 16384)
    def _():
        half_full = length >= CHUNK

        @pl.when(half_full)
        def _():
            run(0, CHUNK // PIECE, False)

        @pl.when(length != CHUNK)
        def _():
            run(pl.multiple_of(jnp.where(half_full, CHUNK, 0), CHUNK), CHUNK // PIECE, True)

    def finish():
        l_old = jnp.sum(total_l[...], axis=0, keepdims=True)
        lse_old = shift[0:1, :] * math.log(2.0) + jnp.log(l_old)
        lse_new = new_lse[0:1, :]
        high = jnp.maximum(lse_old, lse_new)
        f_old = jnp.exp(lse_old - high)
        f_new = jnp.exp(lse_new - high)
        both = f_old + f_new
        o = total_o[...] * (f_old / (l_old * both)) + new_o[...] * (f_new / both)
        lse = jnp.broadcast_to(high + jnp.log(both), (8, 256))
        for target, first in ((keep, mine == 0), (send, mine != 0)):
            target[0:128, :] = jnp.where(first, o[:, 0:128], o[:, 128:256])
            target[128:136, :] = jnp.where(first, lse[:, 0:128], lse[:, 128:256])

    finish()

    @pl.when(jnp.logical_not(jnp.max(total_l[...]) < 1e30))
    def _():
        pieces = lax.div(length + (PIECE - 1), PIECE)
        shift[...] = jnp.full((8, 256), LOW, F32)

        @pl.loop(0, pieces)
        def _(c):
            start = pl.multiple_of(c * PIECE, PIECE)
            top = jnp.max(only_valid(score(start), start), axis=0, keepdims=True)
            shift[...] = jnp.maximum(shift[...], top)

        restart(shift[0:1, :])

        @pl.loop(0, pieces)
        def _(c):
            run(pl.multiple_of(c * PIECE, PIECE), 1, True)

        finish()


def merge_pair_kernel(own, other, copies):
    la, lb = own[128:136, :], other[128:136, :]
    high = jnp.maximum(la, lb)
    fa, fb = jnp.exp(la - high), jnp.exp(lb - high)
    both = fa + fb
    o = (own[0:128, :] * (fa / both)[0:1] + other[0:128, :] * (fb / both)[0:1]).astype(BF16)
    lse = high + jnp.log(both)
    p0 = lse.astype(BF16).astype(F32)
    rest = lse - p0
    p1 = rest.astype(BF16).astype(F32)
    p2 = rest - p1
    row = lax.broadcasted_iota(jnp.int32, (8, LANES), 0)
    tail = jnp.where(row == 0, p0, jnp.where(row == 1, p1, p2))
    tail = jnp.concatenate([tail, jnp.zeros((8, LANES), F32)], axis=0).astype(BF16)
    for j in range(8):
        copies[j, 0:128, :] = o
        copies[j, 128:144, :] = tail


def merge_kernel(parts, attn):
    rows = []
    for j in range(8):
        tail = parts[j, 128:144, :].astype(F32)
        rows.append(tail[0:1] + tail[1:2] + tail[2:3])
    high = functools.reduce(jnp.maximum, rows)
    weights = [jnp.exp(r - high) for r in rows]
    both = functools.reduce(jnp.add, weights)
    total = parts[0, 0:128, :].astype(F32) * (weights[0] / both)
    for j in range(1, 8):
        total += parts[j, 0:128, :].astype(F32) * (weights[j] / both)
    total = jnp.transpose(total)
    for g in range(4):
        attn[:, g * 128 : (g + 1) * 128] = total[g * 32 : (g + 1) * 32].astype(BF16)


def out_half(attn, w_out, half):
    return dot(attn[...], w_out[pl.ds(pl.multiple_of(half * 512, LANES), 512), :])


def out_own_kernel(attn, w_out, part):
    part[...] = out_half(attn, w_out, core_index())


def out_other_kernel(own, attn, w_out, copies):
    part = (own[...] + out_half(attn, w_out, 1 - core_index())).astype(BF16)
    for j in range(8):
        copies[j] = part


def sum_parts(parts):
    total = parts[0].astype(F32)
    for j in range(1, 8):
        total = total + parts[j].astype(F32)
    return total


def gate_up(x, w_gate, w_up, half, target):
    for i in range(2):
        cols = pl.ds(pl.multiple_of(half * 1792 + i * 896, LANES), 896)
        target[:, i * 896 : (i + 1) * 896] = dot(x, w_gate[:, cols]).astype(target.dtype)
        target[:, 1792 + i * 896 : 1792 + (i + 1) * 896] = dot(x, w_up[:, cols]).astype(target.dtype)


def gate_up_send_kernel(parts, resid, gain, w_gate, w_up, branch_out, mid, normed, square, send):
    branch = sum_parts(parts).astype(BF16)
    branch_out[...] = branch
    hidden = (resid[...].astype(F32) + branch.astype(F32)).astype(BF16)
    mid[...] = hidden
    x32 = hidden.astype(F32)
    x = (x32 * gain[...].astype(F32)[None, :]).astype(BF16)
    normed[...] = x
    total = jnp.broadcast_to(jnp.sum(x32 * x32, axis=1, keepdims=True), (32, LANES))
    square[...] = total
    gate_up(x, w_gate, w_up, 1 - core_index(), send)
    send[:, 3584:3712] = lane_split(total)


def gate_up_keep_kernel(normed, branch, w_gate, w_up, keep, attn_out, sem):
    out = pltpu.make_async_copy(branch, attn_out, sem)
    out.start()
    gate_up(normed[...], w_gate, w_up, core_index(), keep)
    out.wait()


def gate_up_pair_kernel(keep, own_square, got, pieces):
    square = own_square[...] + lane_join(got[:, 3584:3712].astype(F32))
    high = square.astype(BF16).astype(F32)
    low = square - high
    for j in range(8):
        rows = slice((j // 2) * 8, (j // 2) * 8 + 8)
        block = []
        for base in (0, 1792):
            cols = slice(base + (j % 2) * 896, base + (j % 2 + 1) * 896)
            block.append(keep[rows, cols] + got[:, cols].astype(F32)[rows])
        pieces[j, :, 0:896] = jnp.concatenate(block, axis=0).astype(BF16)
        pieces[j, :, 896:1024] = jnp.concatenate([high[rows], low[rows]], axis=0).astype(BF16)


def act_kernel(parts, copies):
    total = sum_parts(parts)
    square = (total[0:8] + total[8:16])[:, 896:897]
    inv = lax.rsqrt(square / 8192 + EPS)
    gate = total[0:8, 0:896] * inv
    up = total[8:16, 0:896] * inv
    act = gate / (1.0 + jnp.exp(-gate)) * up
    packed = jnp.concatenate(
        [act[:, 0:512], jnp.concatenate([act[:, 512:896], jnp.zeros((8, LANES), F32)], axis=1)], axis=0
    ).astype(BF16)
    for j in range(8):
        copies[j] = packed


def down(acts, w_down, half):
    total = jnp.zeros((32, 512), F32)
    for ch in range(2):
        wide = []
        for rg in range(4):
            piece = acts[rg * 2 + ch].astype(F32)
            wide.append(jnp.concatenate([piece[0:8], piece[8:16, 0:384]], axis=1))
        act = jnp.concatenate(wide, axis=0).astype(BF16)
        rows = pl.ds(pl.multiple_of(half * 1792 + ch * 896, LANES), 896)
        total += dot(act, w_down[rows, :])
    return total


def down_own_kernel(acts, w_down, part):
    part[...] = down(acts, w_down, core_index())


def down_other_kernel(own, acts, w_down, copies):
    part = (own[...] + down(acts, w_down, 1 - core_index())).astype(BF16)
    for j in range(8):
        copies[j] = part


def final_kernel(parts, mid, layer_out):
    layer_out[...] = (mid[...].astype(F32) + sum_parts(parts)).astype(BF16)


def body(
    resid,
    attn_gain,
    ffn_gain,
    w_query,
    w_key,
    w_value,
    w_out,
    rope_angle,
    positions,
    cache_keys,
    cache_values,
    valid_lengths,
    w_gate,
    w_up,
    w_down,
):
    shape = jax.ShapeDtypeStruct
    near = pltpu.VMEM
    same_core = [[2 * j + c for j in range(8)] for c in range(2)]
    swap = [(i, i ^ 1) for i in range(16)]

    def to_other_core(x):
        return lax.ppermute(x, "seq", swap)

    def over_chips(x):
        return lax.all_to_all(x, "seq", 0, 0, axis_index_groups=same_core)

    def over_tp(x):
        return lax.all_to_all(x, "tp", 0, 0)

    table = near((32, LANES), F32)
    keep, send, cos, sin = call(
        project_kernel,
        (near((32, 768), F32), near((32, 768), F32), table, table),
        [HBM] * 6,
        scratch=[
            pltpu.VMEM((32, 512), BF16),
            pltpu.VMEM((512,), BF16),
            pltpu.VMEM((512, 1024), BF16),
            pltpu.VMEM((2, 512, LANES), BF16),
            pltpu.VMEM((32, 64), F32),
            pltpu.SemaphoreType.DMA((9,)),
        ],
    )(resid, attn_gain, w_query, w_key, w_value, rope_angle)
    copies = call(project_pair_kernel, near((8, 136, LANES), F32), [VMEM] * 2 + [HBM] * 3)(
        keep, to_other_core(send), w_gate, w_up, w_down
    )
    turned = call(rotate_kernel, near((144, LANES), BF16), [VMEM] * 3, scratch=[pltpu.VMEM((32, LANES), F32)])(
        over_chips(copies), cos, sin
    )

    keep, send = call(
        attend_kernel,
        (near((136, LANES), F32), near((136, LANES), F32)),
        [VMEM] * 2 + [SMEM] * 2 + [VMEM] * 2,
        scratch=[
            pltpu.VMEM((256, LANES), BF16),
            pltpu.VMEM((8, 256), F32),
            pltpu.VMEM((8, 256), F32),
            pltpu.VMEM((LANES, 256), F32),
            pltpu.VMEM((LANES, 256), F32),
            pltpu.VMEM((8, 256), F32),
        ],
        limit=24,
    )(turned, to_other_core(turned), positions, valid_lengths, cache_keys, cache_values)
    copies = call(merge_pair_kernel, near((8, 144, LANES), BF16), [VMEM] * 2)(keep, to_other_core(send))
    attn = call(merge_kernel, near((32, 512), BF16), [VMEM])(over_chips(copies))
    got = to_other_core(attn)
    part = call(out_own_kernel, near((32, 512), F32), [VMEM] * 2)(attn, w_out)
    copies = call(out_other_kernel, near((8, 32, 512), BF16), [VMEM] * 3)(part, got, w_out)
    parts = over_tp(copies)

    branch, mid, normed, square, send = call(
        gate_up_send_kernel,
        (near((32, 512), BF16), near((32, 512), BF16), near((32, 512), BF16), table, near((32, 3712), BF16)),
        [VMEM] * 5,
        limit=12,
    )(parts, resid, ffn_gain, w_gate, w_up)
    got = to_other_core(send)
    keep, attn_out = call(
        gate_up_keep_kernel,
        (near((32, 3584), F32), shape((32, 512), BF16)),
        [VMEM] * 4,
        scratch=[pltpu.SemaphoreType.DMA],
        limit=12,
        out_specs=[VMEM, HBM],
    )(normed, branch, w_gate, w_up)
    pieces = call(gate_up_pair_kernel, near((8, 16, 1024), BF16), [VMEM] * 3)(keep, square, got)
    parts = over_chips(pieces)
    copies = call(act_kernel, near((8, 16, 512), BF16), [VMEM])(parts)
    acts = over_chips(copies)
    got = to_other_core(acts)
    part = call(down_own_kernel, near((32, 512), F32), [VMEM] * 2, limit=8)(acts, w_down)
    copies = call(down_other_kernel, near((8, 32, 512), BF16), [VMEM] * 3, limit=8)(part, got, w_down)
    parts = over_tp(copies)
    layer_out = call(final_kernel, shape((32, 512), BF16), [VMEM] * 2)(parts, mid)
    return (attn_out, layer_out)


def solution(mesh):
    in_specs = (
        P(None, "seq"),
        P("seq"),
        P("seq"),
        P("seq", "tp"),
        P("seq", "tp"),
        P("seq", "tp"),
        P("tp", "seq"),
        P(),
        P(),
        P("tp", "seq", None),
        P("tp", "seq", None),
        P("seq"),
        P("seq", "tp"),
        P("seq", "tp"),
        P("tp", "seq"),
    )
    out_specs = (P(None, "seq"), P(None, "seq"))
    return jax.shard_map(body, mesh=mesh, in_specs=in_specs, out_specs=out_specs, check_vma=False)
```

```python
import functools
import math

import jax
import jax.numpy as jnp
from jax import lax
from jax.experimental import pallas as pl
from jax.experimental.pallas import tpu as pltpu
from jax.sharding import PartitionSpec as P

EPS = 1e-05
LOW = -1e30
TINY = 1e-30
FULL = 32766.0
F32 = jnp.float32
BF16 = jnp.bfloat16
LANES = 128
CHUNK = 8192
PIECE = 1024
VMEM = pl.BlockSpec(memory_space=pltpu.VMEM)
SMEM = pl.BlockSpec(memory_space=pltpu.SMEM)
HBM = pl.BlockSpec(memory_space=pltpu.HBM)


def call(kernel, out_shape, in_specs, scratch=(), limit=4, out_specs=None):
    many = isinstance(out_shape, (tuple, list))
    inner = pl.pallas_call(
        kernel,
        out_shape=out_shape,
        in_specs=in_specs,
        out_specs=out_specs or ([VMEM] * len(out_shape) if many else VMEM),
        scratch_shapes=list(scratch),
        compiler_params=pltpu.CompilerParams(vmem_limit_bytes=limit << 20),
    )

    def run(*args):
        return inner(
            *(pltpu.with_memory_space_constraint(x, pltpu.HBM) if s is HBM else x for x, s in zip(args, in_specs))
        )

    return run


def dot(a, b):
    return jnp.dot(a, b, preferred_element_type=F32)


def dot_t(a, b):
    return lax.dot_general(a, b, (((1,), (1,)), ((), ())), preferred_element_type=F32)


def dot_tt(a, b):
    return lax.dot_general(a, b, (((0,), (0,)), ((), ())), preferred_element_type=F32)


def split2(x):
    high = x.astype(BF16)
    return high, (x - high.astype(F32)).astype(BF16)


def lane_split(square):
    high, low = split2(square)
    lane = lax.broadcasted_iota(jnp.int32, square.shape, 1)
    return jnp.where(lane < LANES // 2, high.astype(F32), low.astype(F32)).astype(BF16)


def lane_join(pair):
    return pair + pltpu.roll(pair, LANES // 2, 1)


def core_index():
    return lax.rem(lax.axis_index("seq"), 2)


def chip_index():
    return lax.div(lax.axis_index("seq"), 2)


def project_kernel(
    resid,
    gain,
    w_query,
    w_key,
    w_value,
    angle,
    keep,
    send,
    cos,
    sin,
    x_buf,
    gain_buf,
    q_buf,
    kv_buf,
    angle_buf,
    sems,
):
    mine = core_index()
    pairs = [
        (angle, angle_buf),
        (resid, x_buf),
        (gain, gain_buf),
        (w_key, kv_buf.at[0]),
        (w_value, kv_buf.at[1]),
    ]
    pairs += [(w_query.at[pl.ds(i * 128, 128), :], q_buf.at[pl.ds(i * 128, 128), :]) for i in range(4)]
    loads = [pltpu.make_async_copy(src, dst, sems.at[i]) for i, (src, dst) in enumerate(pairs)]
    for load in loads:
        load.start()
    loads[0].wait()
    cosine, sine = jnp.cos(angle_buf[...]), jnp.sin(angle_buf[...])
    cos[...] = jnp.concatenate([cosine, cosine], axis=1)
    sin[...] = jnp.concatenate([-sine, sine], axis=1)
    loads[1].wait()
    loads[2].wait()
    x32 = x_buf[...].astype(F32)
    x = (x32 * gain_buf[...].astype(F32)[None, :]).astype(BF16)
    square = jnp.broadcast_to(jnp.sum(x32 * x32, axis=1, keepdims=True), (32, LANES))
    loads[3].wait()
    loads[4].wait()
    for target, half in ((keep, mine), (send, 1 - mine)):
        target[:, 512:640] = dot(x, kv_buf[half])
        target[:, 640:768] = square
    total = jnp.zeros((32, 1024), F32)
    for i in range(4):
        loads[5 + i].wait()
        total += dot(x[:, i * 128 : (i + 1) * 128], q_buf[i * 128 : (i + 1) * 128, :])
    first, second = total[:, 0:512], total[:, 512:1024]
    keep[:, 0:512] = jnp.where(mine == 0, first, second)
    send[:, 0:512] = jnp.where(mine == 0, second, first)


def project_pair_kernel(own, other, w1, w2, w3, copies):
    total = own[...] + other[...]
    row_log = jnp.log2(total[:, 640:768] + TINY)
    meta = [jnp.floor(row_log * 256 + 0.5)]
    meta.append(jnp.floor((row_log * 256 - meta[0]) * 16384 + 0.5))
    coded = []
    for cols in (slice(0, 512), slice(512, 640)):
        x = total[:, cols]
        grade = jnp.ceil(jnp.log2(jnp.max(jnp.abs(x), axis=1, keepdims=True) + TINY))
        coded.append(jnp.floor(x * (FULL * jnp.exp2(-grade)) + 0.5))
        meta.append(jnp.broadcast_to(grade, (32, LANES)))
    lane = lax.broadcasted_iota(jnp.int32, (32, LANES), 1)
    last = jnp.where(lane < 2, jnp.where(lane == 0, meta[0], meta[1]), jnp.where(lane == 2, meta[2], meta[3]))
    last = jnp.transpose(jnp.concatenate([last, jnp.zeros((96, LANES), F32)], axis=0))[0:8]
    heads = jnp.concatenate([coded[0][:, g * 128 : (g + 1) * 128] for g in range(4)], axis=0)
    heads = heads.astype(jnp.int32).astype(jnp.int16)
    for j in range(8):
        four = coded[1][j // 2 * 8 : j // 2 * 8 + 8]
        four = pltpu.roll(four, 4, 0) if j % 2 else four
        copies[j, 0:128, :] = heads
        copies[j, 128:144, :] = jnp.concatenate([four, last], axis=0).astype(jnp.int32).astype(jnp.int16)


def rotate_kernel(parts, cos, sin, out, steps):
    tails = [parts[j, 128:144, :].astype(jnp.int32).astype(F32) for j in range(8)]
    square = jnp.zeros((1, LANES), F32)
    for tail in tails:
        square += jnp.exp2(tail[8:9] / 256 + tail[9:10] / (256 * 16384))
    inv = lax.rsqrt(square / 8192 + EPS)
    rows = [jnp.exp2(tail[10:11]) * (inv / FULL) for tail in tails]
    rows += [jnp.exp2(tail[11:12]) * (inv / FULL) for tail in tails]
    turned = jnp.transpose(jnp.concatenate(rows + [jnp.zeros((112, LANES), F32)], axis=0))
    steps[...] = turned[0:32]
    wide = [jnp.broadcast_to(turned[0:32, j : j + 1], (32, LANES)) for j in range(8)]

    for g in range(4):
        x = jnp.zeros((32, LANES), F32)
        for j in range(8):
            head = parts[j, g * 32 : (g + 1) * 32, :].astype(jnp.int32).astype(F32)
            x += head * wide[j]
        out[g * 32 : (g + 1) * 32, :] = (x * cos[...] + pltpu.roll(x, LANES // 2, 1) * sin[...]).astype(BF16)

    chip = chip_index()
    base = pl.ds(pl.multiple_of(lax.div(chip, 2) * 8, 8), 8)

    def four(ref):
        x = ref[base, :]
        return jnp.where(lax.rem(chip, 2) == 0, x, pltpu.roll(x, 4, 0))

    step = four(steps)
    x = jnp.zeros((8, LANES), F32)
    for j in range(8):
        x += tails[j][0:8] * step[:, 8 + j : 9 + j]
    key = x * four(cos) + pltpu.roll(x, LANES // 2, 1) * four(sin)
    x = jnp.where(core_index() == 0, key, x)
    out[128:144, :] = jnp.concatenate([x, jnp.zeros((8, LANES), F32)], axis=0).astype(BF16)


def attend_kernel(
    own, other, positions, valid, keys, values, keep, send, query, shift, total_l, total_o, new_o, new_lse
):
    scale = 128.0**-0.5
    power = scale * 1.4426950408889634
    mine = core_index()
    length = valid[0]

    query[pl.ds(pl.multiple_of(mine * 128, 128), 128), :] = own[0:128, :]
    query[pl.ds(pl.multiple_of((1 - mine) * 128, 128), 128), :] = other[0:128, :]
    q = query[...]
    a, b = own[128:144, :].astype(F32), other[128:144, :].astype(F32)
    k_new = jnp.where(mine == 0, a, b).astype(BF16)
    v_new = jnp.where(mine == 0, b, a).astype(BF16)

    lane = lax.broadcasted_iota(jnp.int32, (8, 256), 1) & 31
    row = lax.broadcasted_iota(jnp.int32, (16, 256), 0)
    of_query = jnp.zeros((8, 256), jnp.int32)
    of_key = jnp.full((16, 256), 1 << 20, jnp.int32)
    for i in range(32):
        of_query = jnp.where(lane == i, positions[i], of_query)
    for i in range(4):
        of_key = jnp.where(row == i, positions[chip_index() * 4 + i], of_key)
    allowed = (of_key <= of_query[0:1, :]) & (mine == 0)
    s_new = jnp.where(allowed, dot_t(k_new, q) * scale, LOW)
    top_new = jnp.max(s_new, axis=0, keepdims=True)
    e_new = jnp.exp(s_new - top_new).astype(BF16)
    l_new = jnp.sum(e_new.astype(F32), axis=0, keepdims=True)
    lse_new = top_new + jnp.log(l_new)
    new_o[...] = dot_tt(v_new, e_new) / l_new
    new_lse[...] = jnp.broadcast_to(lse_new, (8, 256))

    def score(start, count=PIECE):
        return dot_t(keys[0, pl.ds(start, count), :], q)

    def only_valid(s, start):
        slot = lax.broadcasted_iota(jnp.int32, s.shape, 0) + start
        return jnp.where(slot < length, s, LOW)

    def weigh(s, start, carry):
        sums, o = carry
        e = jnp.exp2(s * power - shift[0:1, :]).astype(BF16)
        sums = sums + jnp.sum(e.astype(F32).reshape(PIECE // 8, 8, 256), axis=0)
        return sums, o + dot_tt(values[0, pl.ds(start, PIECE), :], e)

    def run(first, pieces, masked):
        carry = (total_l[...], total_o[...])
        starts = [pl.multiple_of(first + i * PIECE, PIECE) for i in range(pieces)]
        s = score(starts[0])
        for i in range(pieces):
            ahead = score(starts[i + 1]) if i + 1 < pieces else None
            carry = weigh(only_valid(s, starts[i]) if masked else s, starts[i], carry)
            s = ahead
        total_l[...], total_o[...] = carry

    def restart(top):
        shift[...] = jnp.broadcast_to(top * power, (8, 256))
        total_l[...] = jnp.zeros((8, 256), F32)
        total_o[...] = jnp.zeros((LANES, 256), F32)

    restart(jnp.max(only_valid(score(0, 256), 0), axis=0, keepdims=True))

    @pl.when(length == 16384)
    def _():
        run(0, 16384 // PIECE, False)

    @pl.when(length < 16384)
    def _():
        half_full = length >= CHUNK

        @pl.when(half_full)
        def _():
            run(0, CHUNK // PIECE, False)

        @pl.when(length != CHUNK)
        def _():
            run(pl.multiple_of(jnp.where(half_full, CHUNK, 0), CHUNK), CHUNK // PIECE, True)

    def finish():
        l_old = jnp.sum(total_l[...], axis=0, keepdims=True)
        lse_old = shift[0:1, :] * math.log(2.0) + jnp.log(l_old)
        lse_new = new_lse[0:1, :]
        high = jnp.maximum(lse_old, lse_new)
        f_old = jnp.exp(lse_old - high)
        f_new = jnp.exp(lse_new - high)
        both = f_old + f_new
        o = total_o[...] * (f_old / (l_old * both)) + new_o[...] * (f_new / both)
        lse = jnp.broadcast_to(high + jnp.log(both), (8, 256))
        for target, first in ((keep, mine == 0), (send, mine != 0)):
            target[0:128, :] = jnp.where(first, o[:, 0:128], o[:, 128:256])
            target[128:136, :] = jnp.where(first, lse[:, 0:128], lse[:, 128:256])

    finish()

    @pl.when(jnp.logical_not(jnp.max(total_l[...]) < 1e30))
    def _():
        pieces = lax.div(length + (PIECE - 1), PIECE)
        shift[...] = jnp.full((8, 256), LOW, F32)

        @pl.loop(0, pieces)
        def _(c):
            start = pl.multiple_of(c * PIECE, PIECE)
            top = jnp.max(only_valid(score(start), start), axis=0, keepdims=True)
            shift[...] = jnp.maximum(shift[...], top)

        restart(shift[0:1, :])

        @pl.loop(0, pieces)
        def _(c):
            run(pl.multiple_of(c * PIECE, PIECE), 1, True)

        finish()


def merge_pair_kernel(own, other, copies):
    la, lb = own[128:136, :], other[128:136, :]
    high = jnp.maximum(la, lb)
    fa, fb = jnp.exp(la - high), jnp.exp(lb - high)
    both = fa + fb
    o = (own[0:128, :] * (fa / both)[0:1] + other[0:128, :] * (fb / both)[0:1]).astype(BF16)
    lse = high + jnp.log(both)
    p0 = lse.astype(BF16).astype(F32)
    rest = lse - p0
    p1 = rest.astype(BF16).astype(F32)
    p2 = rest - p1
    row = lax.broadcasted_iota(jnp.int32, (8, LANES), 0)
    tail = jnp.where(row == 0, p0, jnp.where(row == 1, p1, p2))
    tail = jnp.concatenate([tail, jnp.zeros((8, LANES), F32)], axis=0).astype(BF16)
    for j in range(8):
        copies[j, 0:128, :] = o
        copies[j, 128:144, :] = tail


def merge_kernel(parts, attn):
    rows = []
    for j in range(8):
        tail = parts[j, 128:144, :].astype(F32)
        rows.append(tail[0:1] + tail[1:2] + tail[2:3])
    high = functools.reduce(jnp.maximum, rows)
    weights = [jnp.exp(r - high) for r in rows]
    both = functools.reduce(jnp.add, weights)
    total = parts[0, 0:128, :].astype(F32) * (weights[0] / both)
    for j in range(1, 8):
        total += parts[j, 0:128, :].astype(F32) * (weights[j] / both)
    total = jnp.transpose(total)
    for g in range(4):
        attn[:, g * 128 : (g + 1) * 128] = total[g * 32 : (g + 1) * 32].astype(BF16)


def out_half(attn, w_out, half):
    return dot(attn[...], w_out[pl.ds(pl.multiple_of(half * 512, LANES), 512), :])


def out_own_kernel(attn, w_out, part):
    part[...] = out_half(attn, w_out, core_index())


def out_other_kernel(own, attn, w_out, copies):
    part = (own[...] + out_half(attn, w_out, 1 - core_index())).astype(BF16)
    for j in range(8):
        copies[j] = part


def sum_parts(parts):
    total = parts[0].astype(F32)
    for j in range(1, 8):
        total = total + parts[j].astype(F32)
    return total


def gate_up(x, w_gate, w_up, half, target):
    for i in range(2):
        cols = pl.ds(pl.multiple_of(half * 1792 + i * 896, LANES), 896)
        target[:, i * 896 : (i + 1) * 896] = dot(x, w_gate[:, cols]).astype(target.dtype)
        target[:, 1792 + i * 896 : 1792 + (i + 1) * 896] = dot(x, w_up[:, cols]).astype(target.dtype)


def gate_up_send_kernel(parts, resid, gain, w_gate, w_up, branch_out, mid, normed, square, send):
    branch = sum_parts(parts).astype(BF16)
    branch_out[...] = branch
    hidden = (resid[...].astype(F32) + branch.astype(F32)).astype(BF16)
    mid[...] = hidden
    x32 = hidden.astype(F32)
    x = (x32 * gain[...].astype(F32)[None, :]).astype(BF16)
    normed[...] = x
    total = jnp.broadcast_to(jnp.sum(x32 * x32, axis=1, keepdims=True), (32, LANES))
    square[...] = total
    gate_up(x, w_gate, w_up, 1 - core_index(), send)
    send[:, 3584:3712] = lane_split(total)


def gate_up_keep_kernel(normed, branch, w_gate, w_up, keep, attn_out, sem):
    out = pltpu.make_async_copy(branch, attn_out, sem)
    out.start()
    gate_up(normed[...], w_gate, w_up, core_index(), keep)
    out.wait()


def gate_up_pair_kernel(keep, own_square, got, pieces):
    square = own_square[...] + lane_join(got[:, 3584:3712].astype(F32))
    high = square.astype(BF16).astype(F32)
    low = square - high
    for j in range(8):
        rows = slice((j // 2) * 8, (j // 2) * 8 + 8)
        block = []
        for base in (0, 1792):
            cols = slice(base + (j % 2) * 896, base + (j % 2 + 1) * 896)
            block.append(keep[rows, cols] + got[:, cols].astype(F32)[rows])
        pieces[j, :, 0:896] = jnp.concatenate(block, axis=0).astype(BF16)
        pieces[j, :, 896:1024] = jnp.concatenate([high[rows], low[rows]], axis=0).astype(BF16)


def act_kernel(parts, copies):
    total = sum_parts(parts)
    square = (total[0:8] + total[8:16])[:, 896:897]
    inv = lax.rsqrt(square / 8192 + EPS)
    gate = total[0:8, 0:896] * inv
    up = total[8:16, 0:896] * inv
    act = gate / (1.0 + jnp.exp(-gate)) * up
    packed = jnp.concatenate(
        [act[:, 0:512], jnp.concatenate([act[:, 512:896], jnp.zeros((8, LANES), F32)], axis=1)], axis=0
    ).astype(BF16)
    for j in range(8):
        copies[j] = packed


def down(acts, w_down, half):
    total = jnp.zeros((32, 512), F32)
    for ch in range(2):
        wide = []
        for rg in range(4):
            piece = acts[rg * 2 + ch].astype(F32)
            wide.append(jnp.concatenate([piece[0:8], piece[8:16, 0:384]], axis=1))
        act = jnp.concatenate(wide, axis=0).astype(BF16)
        rows = pl.ds(pl.multiple_of(half * 1792 + ch * 896, LANES), 896)
        total += dot(act, w_down[rows, :])
    return total


def down_own_kernel(acts, w_down, part):
    part[...] = down(acts, w_down, core_index())


def down_other_kernel(own, acts, w_down, copies):
    part = (own[...] + down(acts, w_down, 1 - core_index())).astype(BF16)
    for j in range(8):
        copies[j] = part


def final_kernel(parts, mid, layer_out):
    layer_out[...] = (mid[...].astype(F32) + sum_parts(parts)).astype(BF16)


def body(
    resid,
    attn_gain,
    ffn_gain,
    w_query,
    w_key,
    w_value,
    w_out,
    rope_angle,
    positions,
    cache_keys,
    cache_values,
    valid_lengths,
    w_gate,
    w_up,
    w_down,
):
    shape = jax.ShapeDtypeStruct
    near = pltpu.VMEM
    same_core = [[2 * j + c for j in range(8)] for c in range(2)]
    swap = [(i, i ^ 1) for i in range(16)]

    def to_other_core(x):
        return lax.ppermute(x, "seq", swap)

    def over_chips(x):
        return lax.all_to_all(x, "seq", 0, 0, axis_index_groups=same_core)

    def over_tp(x):
        return lax.all_to_all(x, "tp", 0, 0)

    table = near((32, LANES), F32)
    keep, send, cos, sin = call(
        project_kernel,
        (near((32, 768), F32), near((32, 768), F32), table, table),
        [HBM] * 6,
        scratch=[
            pltpu.VMEM((32, 512), BF16),
            pltpu.VMEM((512,), BF16),
            pltpu.VMEM((512, 1024), BF16),
            pltpu.VMEM((2, 512, LANES), BF16),
            pltpu.VMEM((32, 64), F32),
            pltpu.SemaphoreType.DMA((9,)),
        ],
    )(resid, attn_gain, w_query, w_key, w_value, rope_angle)
    copies = call(project_pair_kernel, near((8, 144, LANES), jnp.int16), [VMEM] * 2 + [HBM] * 3)(
        keep, to_other_core(send), w_gate, w_up, w_down
    )
    turned = call(rotate_kernel, near((144, LANES), BF16), [VMEM] * 3, scratch=[pltpu.VMEM((32, LANES), F32)])(
        over_chips(copies), cos, sin
    )

    keep, send = call(
        attend_kernel,
        (near((136, LANES), F32), near((136, LANES), F32)),
        [VMEM] * 2 + [SMEM] * 2 + [VMEM] * 2,
        scratch=[
            pltpu.VMEM((256, LANES), BF16),
            pltpu.VMEM((8, 256), F32),
            pltpu.VMEM((8, 256), F32),
            pltpu.VMEM((LANES, 256), F32),
            pltpu.VMEM((LANES, 256), F32),
            pltpu.VMEM((8, 256), F32),
        ],
        limit=24,
    )(turned, to_other_core(turned), positions, valid_lengths, cache_keys, cache_values)
    copies = call(merge_pair_kernel, near((8, 144, LANES), BF16), [VMEM] * 2)(keep, to_other_core(send))
    attn = call(merge_kernel, near((32, 512), BF16), [VMEM])(over_chips(copies))
    got = to_other_core(attn)
    part = call(out_own_kernel, near((32, 512), F32), [VMEM] * 2)(attn, w_out)
    copies = call(out_other_kernel, near((8, 32, 512), BF16), [VMEM] * 3)(part, got, w_out)
    parts = over_tp(copies)

    branch, mid, normed, square, send = call(
        gate_up_send_kernel,
        (near((32, 512), BF16), near((32, 512), BF16), near((32, 512), BF16), table, near((32, 3712), BF16)),
        [VMEM] * 5,
        limit=12,
    )(parts, resid, ffn_gain, w_gate, w_up)
    got = to_other_core(send)
    keep, attn_out = call(
        gate_up_keep_kernel,
        (near((32, 3584), F32), shape((32, 512), BF16)),
        [VMEM] * 4,
        scratch=[pltpu.SemaphoreType.DMA],
        limit=12,
        out_specs=[VMEM, HBM],
    )(normed, branch, w_gate, w_up)
    pieces = call(gate_up_pair_kernel, near((8, 16, 1024), BF16), [VMEM] * 3)(keep, square, got)
    parts = over_chips(pieces)
    copies = call(act_kernel, near((8, 16, 512), BF16), [VMEM])(parts)
    acts = over_chips(copies)
    got = to_other_core(acts)
    part = call(down_own_kernel, near((32, 512), F32), [VMEM] * 2, limit=8)(acts, w_down)
    copies = call(down_other_kernel, near((8, 32, 512), BF16), [VMEM] * 3, limit=8)(part, got, w_down)
    parts = over_tp(copies)
    layer_out = call(final_kernel, shape((32, 512), BF16), [VMEM] * 2)(parts, mid)
    return (attn_out, layer_out)


def solution(mesh):
    in_specs = (
        P(None, "seq"),
        P("seq"),
        P("seq"),
        P("seq", "tp"),
        P("seq", "tp"),
        P("seq", "tp"),
        P("tp", "seq"),
        P(),
        P(),
        P("tp", "seq", None),
        P("tp", "seq", None),
        P("seq"),
        P("seq", "tp"),
        P("seq", "tp"),
        P("tp", "seq"),
    )
    out_specs = (P(None, "seq"), P(None, "seq"))
    return jax.shard_map(body, mesh=mesh, in_specs=in_specs, out_specs=out_specs, check_vma=False)
```

```python
import functools
import math

import jax
import jax.numpy as jnp
from jax import lax
from jax.experimental import pallas as pl
from jax.experimental.pallas import tpu as pltpu
from jax.sharding import PartitionSpec as P

EPS = 1e-05
LOW = -1e30
TINY = 1e-30
FULL = 32766.0
F32 = jnp.float32
BF16 = jnp.bfloat16
LANES = 128
CHUNK = 8192
PIECE = 1024
VMEM = pl.BlockSpec(memory_space=pltpu.VMEM)
SMEM = pl.BlockSpec(memory_space=pltpu.SMEM)
HBM = pl.BlockSpec(memory_space=pltpu.HBM)


def call(kernel, out_shape, in_specs, scratch=(), limit=4, out_specs=None):
    many = isinstance(out_shape, (tuple, list))
    inner = pl.pallas_call(
        kernel,
        out_shape=out_shape,
        in_specs=in_specs,
        out_specs=out_specs or ([VMEM] * len(out_shape) if many else VMEM),
        scratch_shapes=list(scratch),
        compiler_params=pltpu.CompilerParams(vmem_limit_bytes=limit << 20),
    )

    def run(*args):
        return inner(
            *(pltpu.with_memory_space_constraint(x, pltpu.HBM) if s is HBM else x for x, s in zip(args, in_specs))
        )

    return run


def dot(a, b):
    return jnp.dot(a, b, preferred_element_type=F32)


def dot_t(a, b):
    return lax.dot_general(a, b, (((1,), (1,)), ((), ())), preferred_element_type=F32)


def dot_tt(a, b):
    return lax.dot_general(a, b, (((0,), (0,)), ((), ())), preferred_element_type=F32)


def split2(x):
    high = x.astype(BF16)
    return high, (x - high.astype(F32)).astype(BF16)


def lane_split(square):
    high, low = split2(square)
    lane = lax.broadcasted_iota(jnp.int32, square.shape, 1)
    return jnp.where(lane < LANES // 2, high.astype(F32), low.astype(F32)).astype(BF16)


def lane_join(pair):
    return pair + pltpu.roll(pair, LANES // 2, 1)


def core_index():
    return lax.rem(lax.axis_index("seq"), 2)


def chip_index():
    return lax.div(lax.axis_index("seq"), 2)


def project_kernel(
    resid,
    gain,
    w_query,
    w_key,
    w_value,
    angle,
    keep,
    send,
    cos,
    sin,
    x_buf,
    gain_buf,
    q_buf,
    kv_buf,
    angle_buf,
    sems,
):
    mine = core_index()
    pairs = [
        (angle, angle_buf),
        (resid, x_buf),
        (gain, gain_buf),
        (w_key, kv_buf.at[0]),
        (w_value, kv_buf.at[1]),
    ]
    pairs += [(w_query.at[pl.ds(i * 128, 128), :], q_buf.at[pl.ds(i * 128, 128), :]) for i in range(4)]
    loads = [pltpu.make_async_copy(src, dst, sems.at[i]) for i, (src, dst) in enumerate(pairs)]
    for load in loads:
        load.start()
    loads[0].wait()
    cosine, sine = jnp.cos(angle_buf[...]), jnp.sin(angle_buf[...])
    cos[...] = jnp.concatenate([cosine, cosine], axis=1)
    sin[...] = jnp.concatenate([-sine, sine], axis=1)
    loads[1].wait()
    loads[2].wait()
    x32 = x_buf[...].astype(F32)
    x = (x32 * gain_buf[...].astype(F32)[None, :]).astype(BF16)
    square = jnp.broadcast_to(jnp.sum(x32 * x32, axis=1, keepdims=True), (32, LANES))
    loads[3].wait()
    loads[4].wait()
    for target, half in ((keep, mine), (send, 1 - mine)):
        target[:, 512:640] = dot(x, kv_buf[half])
        target[:, 640:768] = square
    total = jnp.zeros((32, 1024), F32)
    for i in range(4):
        loads[5 + i].wait()
        total += dot(x[:, i * 128 : (i + 1) * 128], q_buf[i * 128 : (i + 1) * 128, :])
    first, second = total[:, 0:512], total[:, 512:1024]
    keep[:, 0:512] = jnp.where(mine == 0, first, second)
    send[:, 0:512] = jnp.where(mine == 0, second, first)


def project_pair_kernel(own, other, w1, w2, w3, copies):
    total = own[...] + other[...]
    row_log = jnp.log2(total[:, 640:768] + TINY)
    meta = [jnp.floor(row_log * 256 + 0.5)]
    meta.append(jnp.floor((row_log * 256 - meta[0]) * 16384 + 0.5))
    coded = []
    for cols in (slice(0, 512), slice(512, 640)):
        x = total[:, cols]
        grade = jnp.ceil(jnp.log2(jnp.max(jnp.abs(x), axis=1, keepdims=True) + TINY))
        coded.append(jnp.floor(x * (FULL * jnp.exp2(-grade)) + 0.5))
        meta.append(jnp.broadcast_to(grade, (32, LANES)))
    lane = lax.broadcasted_iota(jnp.int32, (32, LANES), 1)
    last = jnp.where(lane < 2, jnp.where(lane == 0, meta[0], meta[1]), jnp.where(lane == 2, meta[2], meta[3]))
    last = jnp.transpose(jnp.concatenate([last, jnp.zeros((96, LANES), F32)], axis=0))[0:8]
    heads = jnp.concatenate([coded[0][:, g * 128 : (g + 1) * 128] for g in range(4)], axis=0)
    heads = heads.astype(jnp.int32).astype(jnp.int16)
    for j in range(8):
        four = coded[1][j // 2 * 8 : j // 2 * 8 + 8]
        four = pltpu.roll(four, 4, 0) if j % 2 else four
        copies[j, 0:128, :] = heads
        copies[j, 128:144, :] = jnp.concatenate([four, last], axis=0).astype(jnp.int32).astype(jnp.int16)


def rotate_kernel(parts, cos, sin, out, steps):
    tails = [parts[j, 128:144, :].astype(jnp.int32).astype(F32) for j in range(8)]
    square = jnp.zeros((1, LANES), F32)
    for tail in tails:
        square += jnp.exp2(tail[8:9] / 256 + tail[9:10] / (256 * 16384))
    inv = lax.rsqrt(square / 8192 + EPS)
    rows = [jnp.exp2(tail[10:11]) * (inv / FULL) for tail in tails]
    rows += [jnp.exp2(tail[11:12]) * (inv / FULL) for tail in tails]
    turned = jnp.transpose(jnp.concatenate(rows + [jnp.zeros((112, LANES), F32)], axis=0))
    steps[...] = turned[0:32]
    wide = [jnp.broadcast_to(turned[0:32, j : j + 1], (32, LANES)) for j in range(8)]

    for g in range(4):
        x = jnp.zeros((32, LANES), F32)
        for j in range(8):
            head = parts[j, g * 32 : (g + 1) * 32, :].astype(jnp.int32).astype(F32)
            x += head * wide[j]
        out[g * 32 : (g + 1) * 32, :] = (x * cos[...] + pltpu.roll(x, LANES // 2, 1) * sin[...]).astype(BF16)

    chip = chip_index()
    base = pl.ds(pl.multiple_of(lax.div(chip, 2) * 8, 8), 8)

    def four(ref):
        x = ref[base, :]
        return jnp.where(lax.rem(chip, 2) == 0, x, pltpu.roll(x, 4, 0))

    step = four(steps)
    x = jnp.zeros((8, LANES), F32)
    for j in range(8):
        x += tails[j][0:8] * step[:, 8 + j : 9 + j]
    key = x * four(cos) + pltpu.roll(x, LANES // 2, 1) * four(sin)
    x = jnp.where(core_index() == 0, key, x)
    out[128:144, :] = jnp.concatenate([x, jnp.zeros((8, LANES), F32)], axis=0).astype(BF16)


def attend_kernel(
    own, other, positions, valid, keys, values, keep, send, query, shift, total_l, total_o, new_o, new_lse
):
    scale = 128.0**-0.5
    power = scale * 1.4426950408889634
    mine = core_index()
    length = valid[0]

    query[pl.ds(pl.multiple_of(mine * 128, 128), 128), :] = own[0:128, :]
    query[pl.ds(pl.multiple_of((1 - mine) * 128, 128), 128), :] = other[0:128, :]
    q = query[...]
    a, b = own[128:144, :].astype(F32), other[128:144, :].astype(F32)
    k_new = jnp.where(mine == 0, a, b).astype(BF16)
    v_new = jnp.where(mine == 0, b, a).astype(BF16)

    lane = lax.broadcasted_iota(jnp.int32, (8, 256), 1) & 31
    row = lax.broadcasted_iota(jnp.int32, (16, 256), 0)
    of_query = jnp.zeros((8, 256), jnp.int32)
    of_key = jnp.full((16, 256), 1 << 20, jnp.int32)
    for i in range(32):
        of_query = jnp.where(lane == i, positions[i], of_query)
    for i in range(4):
        of_key = jnp.where(row == i, positions[chip_index() * 4 + i], of_key)
    allowed = (of_key <= of_query[0:1, :]) & (mine == 0)
    s_new = jnp.where(allowed, dot_t(k_new, q) * scale, LOW)
    top_new = jnp.max(s_new, axis=0, keepdims=True)
    e_new = jnp.exp(s_new - top_new).astype(BF16)
    l_new = jnp.sum(e_new.astype(F32), axis=0, keepdims=True)
    lse_new = top_new + jnp.log(l_new)
    new_o[...] = dot_tt(v_new, e_new) / l_new
    new_lse[...] = jnp.broadcast_to(lse_new, (8, 256))

    def score(start, count=PIECE):
        return dot_t(keys[0, pl.ds(start, count), :], q)

    def only_valid(s, start):
        slot = lax.broadcasted_iota(jnp.int32, s.shape, 0) + start
        return jnp.where(slot < length, s, LOW)

    def weigh(s, start, carry):
        sums, o = carry
        e = jnp.exp2(s * power - shift[0:1, :]).astype(BF16)
        sums = sums + jnp.sum(e.astype(F32).reshape(PIECE // 8, 8, 256), axis=0)
        return sums, o + dot_tt(values[0, pl.ds(start, PIECE), :], e)

    def run(first, pieces, masked):
        carry = (total_l[...], total_o[...])
        starts = [pl.multiple_of(first + i * PIECE, PIECE) for i in range(pieces)]
        s = score(starts[0])
        for i in range(pieces):
            ahead = score(starts[i + 1]) if i + 1 < pieces else None
            carry = weigh(only_valid(s, starts[i]) if masked else s, starts[i], carry)
            s = ahead
        total_l[...], total_o[...] = carry

    def restart(top):
        shift[...] = jnp.broadcast_to(top * power, (8, 256))
        total_l[...] = jnp.zeros((8, 256), F32)
        total_o[...] = jnp.zeros((LANES, 256), F32)

    restart(jnp.max(only_valid(score(0, 128), 0), axis=0, keepdims=True))

    @pl.when(length == 16384)
    def _():
        run(0, 16384 // PIECE, False)

    @pl.when(length < 16384)
    def _():
        half_full = length >= CHUNK

        @pl.when(half_full)
        def _():
            run(0, CHUNK // PIECE, False)

        @pl.when(length != CHUNK)
        def _():
            run(pl.multiple_of(jnp.where(half_full, CHUNK, 0), CHUNK), CHUNK // PIECE, True)

    def finish():
        l_old = jnp.sum(total_l[...], axis=0, keepdims=True)
        lse_old = shift[0:1, :] * math.log(2.0) + jnp.log(l_old)
        lse_new = new_lse[0:1, :]
        high = jnp.maximum(lse_old, lse_new)
        f_old = jnp.exp(lse_old - high)
        f_new = jnp.exp(lse_new - high)
        both = f_old + f_new
        o = total_o[...] * (f_old / (l_old * both)) + new_o[...] * (f_new / both)
        lse = jnp.broadcast_to(high + jnp.log(both), (8, 256))
        for target, first in ((keep, mine == 0), (send, mine != 0)):
            target[0:128, :] = jnp.where(first, o[:, 0:128], o[:, 128:256])
            target[128:136, :] = jnp.where(first, lse[:, 0:128], lse[:, 128:256])

    finish()

    @pl.when(jnp.logical_not(jnp.max(total_l[...]) < 1e30))
    def _():
        pieces = lax.div(length + (PIECE - 1), PIECE)
        shift[...] = jnp.full((8, 256), LOW, F32)

        @pl.loop(0, pieces)
        def _(c):
            start = pl.multiple_of(c * PIECE, PIECE)
            top = jnp.max(only_valid(score(start), start), axis=0, keepdims=True)
            shift[...] = jnp.maximum(shift[...], top)

        restart(shift[0:1, :])

        @pl.loop(0, pieces)
        def _(c):
            run(pl.multiple_of(c * PIECE, PIECE), 1, True)

        finish()


def merge_pair_kernel(own, other, copies):
    la, lb = own[128:136, :], other[128:136, :]
    high = jnp.maximum(la, lb)
    fa, fb = jnp.exp(la - high), jnp.exp(lb - high)
    both = fa + fb
    o = (own[0:128, :] * (fa / both)[0:1] + other[0:128, :] * (fb / both)[0:1]).astype(BF16)
    lse = high + jnp.log(both)
    p0 = lse.astype(BF16).astype(F32)
    rest = lse - p0
    p1 = rest.astype(BF16).astype(F32)
    p2 = rest - p1
    row = lax.broadcasted_iota(jnp.int32, (8, LANES), 0)
    tail = jnp.where(row == 0, p0, jnp.where(row == 1, p1, p2))
    tail = jnp.concatenate([tail, jnp.zeros((8, LANES), F32)], axis=0).astype(BF16)
    for j in range(8):
        copies[j, 0:128, :] = o
        copies[j, 128:144, :] = tail


def merge_kernel(parts, attn):
    rows = []
    for j in range(8):
        tail = parts[j, 128:144, :].astype(F32)
        rows.append(tail[0:1] + tail[1:2] + tail[2:3])
    high = functools.reduce(jnp.maximum, rows)
    weights = [jnp.exp(r - high) for r in rows]
    both = functools.reduce(jnp.add, weights)
    total = parts[0, 0:128, :].astype(F32) * (weights[0] / both)
    for j in range(1, 8):
        total += parts[j, 0:128, :].astype(F32) * (weights[j] / both)
    total = jnp.transpose(total)
    for g in range(4):
        attn[:, g * 128 : (g + 1) * 128] = total[g * 32 : (g + 1) * 32].astype(BF16)


def out_kernel(own, other, w_out, copies):
    mine = core_index()
    total = jnp.zeros((32, 512), F32)
    for source, half in ((own, mine), (other, 1 - mine)):
        total += dot(source[...], w_out[pl.ds(pl.multiple_of(half * 512, LANES), 512), :])
    part = total.astype(BF16)
    for j in range(8):
        copies[j] = part


def sum_parts(parts):
    total = parts[0].astype(F32)
    for j in range(1, 8):
        total = total + parts[j].astype(F32)
    return total


def gate_up(x, w_gate, w_up, half, target):
    for i in range(2):
        cols = pl.ds(pl.multiple_of(half * 1792 + i * 896, LANES), 896)
        target[:, i * 896 : (i + 1) * 896] = dot(x, w_gate[:, cols]).astype(target.dtype)
        target[:, 1792 + i * 896 : 1792 + (i + 1) * 896] = dot(x, w_up[:, cols]).astype(target.dtype)


def gate_up_send_kernel(parts, resid, gain, w_gate, w_up, branch_out, mid, normed, square, send):
    branch = sum_parts(parts).astype(BF16)
    branch_out[...] = branch
    hidden = (resid[...].astype(F32) + branch.astype(F32)).astype(BF16)
    mid[...] = hidden
    x32 = hidden.astype(F32)
    x = (x32 * gain[...].astype(F32)[None, :]).astype(BF16)
    normed[...] = x
    total = jnp.broadcast_to(jnp.sum(x32 * x32, axis=1, keepdims=True), (32, LANES))
    square[...] = total
    gate_up(x, w_gate, w_up, 1 - core_index(), send)
    send[:, 3584:3712] = lane_split(total)


def gate_up_keep_kernel(normed, branch, w_gate, w_up, keep, attn_out, sem):
    out = pltpu.make_async_copy(branch, attn_out, sem)
    out.start()
    gate_up(normed[...], w_gate, w_up, core_index(), keep)
    out.wait()


def gate_up_pair_kernel(keep, own_square, got, pieces):
    square = own_square[...] + lane_join(got[:, 3584:3712].astype(F32))
    high = square.astype(BF16).astype(F32)
    low = square - high
    for j in range(8):
        rows = slice((j // 2) * 8, (j // 2) * 8 + 8)
        block = []
        for base in (0, 1792):
            cols = slice(base + (j % 2) * 896, base + (j % 2 + 1) * 896)
            block.append(keep[rows, cols] + got[:, cols].astype(F32)[rows])
        pieces[j, :, 0:896] = jnp.concatenate(block, axis=0).astype(BF16)
        pieces[j, :, 896:1024] = jnp.concatenate([high[rows], low[rows]], axis=0).astype(BF16)


def act_kernel(parts, copies):
    total = sum_parts(parts)
    square = (total[0:8] + total[8:16])[:, 896:897]
    inv = lax.rsqrt(square / 8192 + EPS)
    gate = total[0:8, 0:896] * inv
    up = total[8:16, 0:896] * inv
    act = gate / (1.0 + jnp.exp(-gate)) * up
    packed = jnp.concatenate(
        [act[:, 0:512], jnp.concatenate([act[:, 512:896], jnp.zeros((8, LANES), F32)], axis=1)], axis=0
    ).astype(BF16)
    for j in range(8):
        copies[j] = packed


def down(acts, w_down, half):
    total = jnp.zeros((32, 512), F32)
    for ch in range(2):
        wide = []
        for rg in range(4):
            piece = acts[rg * 2 + ch].astype(F32)
            wide.append(jnp.concatenate([piece[0:8], piece[8:16, 0:384]], axis=1))
        act = jnp.concatenate(wide, axis=0).astype(BF16)
        rows = pl.ds(pl.multiple_of(half * 1792 + ch * 896, LANES), 896)
        total += dot(act, w_down[rows, :])
    return total


def down_own_kernel(acts, w_down, part):
    part[...] = down(acts, w_down, core_index())


def down_other_kernel(own, acts, w_down, copies):
    part = (own[...] + down(acts, w_down, 1 - core_index())).astype(BF16)
    for j in range(8):
        copies[j] = part


def final_kernel(parts, mid, layer_out):
    layer_out[...] = (mid[...].astype(F32) + sum_parts(parts)).astype(BF16)


def body(
    resid,
    attn_gain,
    ffn_gain,
    w_query,
    w_key,
    w_value,
    w_out,
    rope_angle,
    positions,
    cache_keys,
    cache_values,
    valid_lengths,
    w_gate,
    w_up,
    w_down,
):
    shape = jax.ShapeDtypeStruct
    near = pltpu.VMEM
    same_core = [[2 * j + c for j in range(8)] for c in range(2)]
    swap = [(i, i ^ 1) for i in range(16)]

    def to_other_core(x):
        return lax.ppermute(x, "seq", swap)

    def over_chips(x):
        return lax.all_to_all(x, "seq", 0, 0, axis_index_groups=same_core)

    def over_tp(x):
        return lax.all_to_all(x, "tp", 0, 0)

    table = near((32, LANES), F32)
    keep, send, cos, sin = call(
        project_kernel,
        (near((32, 768), F32), near((32, 768), F32), table, table),
        [HBM] * 6,
        scratch=[
            pltpu.VMEM((32, 512), BF16),
            pltpu.VMEM((512,), BF16),
            pltpu.VMEM((512, 1024), BF16),
            pltpu.VMEM((2, 512, LANES), BF16),
            pltpu.VMEM((32, 64), F32),
            pltpu.SemaphoreType.DMA((9,)),
        ],
    )(resid, attn_gain, w_query, w_key, w_value, rope_angle)
    copies = call(project_pair_kernel, near((8, 144, LANES), jnp.int16), [VMEM] * 2 + [HBM] * 3)(
        keep, to_other_core(send), w_gate, w_up, w_down
    )
    turned = call(rotate_kernel, near((144, LANES), BF16), [VMEM] * 3, scratch=[pltpu.VMEM((32, LANES), F32)])(
        over_chips(copies), cos, sin
    )

    keep, send = call(
        attend_kernel,
        (near((136, LANES), F32), near((136, LANES), F32)),
        [VMEM] * 2 + [SMEM] * 2 + [VMEM] * 2,
        scratch=[
            pltpu.VMEM((256, LANES), BF16),
            pltpu.VMEM((8, 256), F32),
            pltpu.VMEM((8, 256), F32),
            pltpu.VMEM((LANES, 256), F32),
            pltpu.VMEM((LANES, 256), F32),
            pltpu.VMEM((8, 256), F32),
        ],
        limit=24,
    )(turned, to_other_core(turned), positions, valid_lengths, cache_keys, cache_values)
    copies = call(merge_pair_kernel, near((8, 144, LANES), BF16), [VMEM] * 2)(keep, to_other_core(send))
    attn = call(merge_kernel, near((32, 512), BF16), [VMEM])(over_chips(copies))
    copies = call(out_kernel, near((8, 32, 512), BF16), [VMEM] * 3)(attn, to_other_core(attn), w_out)
    parts = over_tp(copies)

    branch, mid, normed, square, send = call(
        gate_up_send_kernel,
        (near((32, 512), BF16), near((32, 512), BF16), near((32, 512), BF16), table, near((32, 3712), BF16)),
        [VMEM] * 5,
        limit=12,
    )(parts, resid, ffn_gain, w_gate, w_up)
    got = to_other_core(send)
    keep, attn_out = call(
        gate_up_keep_kernel,
        (near((32, 3584), F32), shape((32, 512), BF16)),
        [VMEM] * 4,
        scratch=[pltpu.SemaphoreType.DMA],
        limit=12,
        out_specs=[VMEM, HBM],
    )(normed, branch, w_gate, w_up)
    pieces = call(gate_up_pair_kernel, near((8, 16, 1024), BF16), [VMEM] * 3)(keep, square, got)
    parts = over_chips(pieces)
    copies = call(act_kernel, near((8, 16, 512), BF16), [VMEM])(parts)
    acts = over_chips(copies)
    got = to_other_core(acts)
    part = call(down_own_kernel, near((32, 512), F32), [VMEM] * 2, limit=8)(acts, w_down)
    copies = call(down_other_kernel, near((8, 32, 512), BF16), [VMEM] * 3, limit=8)(part, got, w_down)
    parts = over_tp(copies)
    layer_out = call(final_kernel, shape((32, 512), BF16), [VMEM] * 2)(parts, mid)
    return (attn_out, layer_out)


def solution(mesh):
    in_specs = (
        P(None, "seq"),
        P("seq"),
        P("seq"),
        P("seq", "tp"),
        P("seq", "tp"),
        P("seq", "tp"),
        P("tp", "seq"),
        P(),
        P(),
        P("tp", "seq", None),
        P("tp", "seq", None),
        P("seq"),
        P("seq", "tp"),
        P("seq", "tp"),
        P("tp", "seq"),
    )
    out_specs = (P(None, "seq"), P(None, "seq"))
    return jax.shard_map(body, mesh=mesh, in_specs=in_specs, out_specs=out_specs, check_vma=False)
```
